32 devices in a mesh: section: 2 (over core), seq: 4 (over z), wshard: 4 (over y, x).
Axes of the slice: x: 2, y: 2, z: 4, core: 2. Of those that a mesh axis runs over, the one named last changes fastest.
Arguments:
- inputs: bfloat16 [4, 4, 1024, 1024], P(None, 'wshard', 'seq'), may hold values from -6 to 6
- seq_lengths: int32 [4, 4], replicated, may hold values from 128 to 1024, as said below
- cotangent: bfloat16 [4, 4, 1024, 1024], P(None, 'wshard', 'seq'), may hold values from -6 to 6
- norm_gain: float32 [2, 1024], P('section'), may hold values from 0.5 to 1.5
- in_weight: bfloat16 [2, 1024, 4384], P('section', ('seq', 'wshard')), may hold values from -0.1875 to 0.1875
- conv_weight: float32 [2, 4, 2304], P('section'), may hold values from -3 to 3
- conv_bias: float32 [2, 2304], P('section'), may hold values from -3 to 3
- dt_bias: float32 [2, 32], P('section'), may hold values from -7 to -2.5
- a_log: float32 [2, 32], P('section'), may hold values from -2.5 to 1.2
- d_skip: float32 [2, 32], P('section'), may hold values from 0.5 to 1.5
- gated_gain: float32 [2, 2048], P('section'), may hold values from 0.5 to 1.5
- out_weight: bfloat16 [2, 2048, 1024], P('section', ('seq', 'wshard')), may hold values from -0.125 to 0.125
Outputs:
- acts: bfloat16 [2, 4, 4, 1024, 1024], P('section', None, 'wshard', 'seq')
- grad_in: bfloat16 [2, 4, 4, 1024, 1024], P('section', None, 'wshard', 'seq')
- grad_norm_gain: float32 [2, 1024], P('section')
- grad_in_weight: float32 [2, 1024, 4384], P('section', ('seq', 'wshard'))
- grad_conv_weight: float32 [2, 4, 2304], P('section')
- grad_conv_bias: float32 [2, 2304], P('section')
- grad_dt_bias: float32 [2, 32], P('section')
- grad_a_log: float32 [2, 32], P('section')
- grad_d_skip: float32 [2, 32], P('section')
- grad_gated_gain: float32 [2, 2048], P('section')
- grad_out_weight: float32 [2, 2048, 1024], P('section', ('seq', 'wshard'))
The draws below stay inside these ranges and needn't reach their ends.
Inputs may be any that keep to these rules, and one draw needn't show every extreme that they name: `seq_lengths`: in each column one entry equals 1024, which row is drawn; the others are at least 128.
All inputs are finite; a program needn't handle non-finite values.
Results may differ from the reference program's by a relative error of at most 0.015.
Values may be sent and summed in bfloat16 or wider, within the bound.
No kernel may reach another device: no remote copies, remote signals or barrier semaphores. Data moves between devices by JAX's collectives and lax.ppermute only.
A program may use at most 384 MiB of HBM per device.

```python
import jax
import jax.numpy as jnp
from jax import lax

D = 1024
DIN = 2048
HEADS = 32
CONV = 4
SPAN = 256
MB = 4
SEQ_LEN = 1024
CH = 2304
PROJ = 4384
N_SEQ = 4
N_WSHARD = 4


def draw_seq_lengths(key, part):
    key = jax.random.fold_in(key, 11)
    key_len, key_full = jax.random.split(key)
    drawn = jax.random.randint(key_len, (MB, N_WSHARD), SEQ_LEN // 8, SEQ_LEN + 1)
    full_row = jax.random.randint(key_full, (N_WSHARD,), 0, MB)
    row_ids = jnp.arange(MB)[:, None]
    return jnp.where(row_ids == full_row[None, :], SEQ_LEN, drawn).astype(jnp.int32)


def levels(stream_key, extent, shards, least, largest):
    level = 1.0
    for dim, parts in shards:
        heights = jax.random.uniform(jax.random.fold_in(jax.random.fold_in(stream_key, 6), dim), (parts,), jnp.float32, least / len(shards), largest / len(shards))
        level = level * jnp.repeat(jnp.exp(heights), extent[dim] // parts).reshape((-1,) + (1,) * (len(extent) - 1 - dim))
    return level


def centred(rng, dims, spread, bound, shards=(), kind=jnp.bfloat16):
    level = levels(rng, dims, shards, -0.22, 0.18) if shards else 1.0
    values = jax.random.normal(rng, dims, jnp.float32) * spread * level
    return jnp.minimum(jnp.maximum(values, -bound), bound).astype(kind)


def setup_inputs(seed: int = 0) -> dict:
    arg_keys = jax.random.split(jax.random.key(seed), 13)
    return {
        "inputs": centred(arg_keys[0], (MB, N_WSHARD, SEQ_LEN, D), 1.0, 6.0, ((1, 4), (2, 4))),
        "seq_lengths": draw_seq_lengths(jax.random.fold_in(arg_keys[12], 71), 0),
        "cotangent": centred(arg_keys[2], (MB, N_WSHARD, SEQ_LEN, D), 1.0, 6.0, ((1, 4), (2, 4))),
        "norm_gain": jnp.clip(0.5 + 1.0 * jax.random.uniform(arg_keys[3], (2, D), jnp.float32) ** levels(arg_keys[3], (2, D), ((0, 2),), -0.2, 0.2), 0.5, 1.5),
        "in_weight": centred(arg_keys[4], (2, D, PROJ), D ** -0.5, 0.1875, ((0, 2), (1, 16))),
        "conv_weight": centred(arg_keys[5], (2, CONV, CH), CONV ** -0.5, 3.0, ((0, 2),), jnp.float32),
        "conv_bias": centred(arg_keys[6], (2, CH), 0.5, 3.0, ((0, 2),), jnp.float32),
        "dt_bias": jnp.clip(-7.0 + 4.5 * jax.random.uniform(arg_keys[7], (2, HEADS), jnp.float32) ** levels(arg_keys[7], (2, HEADS), ((0, 2),), -0.2, 0.2), -7.0, -2.5),
        "a_log": jnp.clip(-2.5 + 3.7 * jax.random.uniform(arg_keys[8], (2, HEADS), jnp.float32) ** levels(arg_keys[8], (2, HEADS), ((0, 2),), -0.2, 0.2), -2.5, 1.2),
        "d_skip": jnp.clip(0.5 + 1.0 * jax.random.uniform(arg_keys[9], (2, HEADS), jnp.float32) ** levels(arg_keys[9], (2, HEADS), ((0, 2),), -0.2, 0.2), 0.5, 1.5),
        "gated_gain": jnp.clip(0.5 + 1.0 * jax.random.uniform(arg_keys[10], (2, DIN), jnp.float32) ** levels(arg_keys[10], (2, DIN), ((0, 2),), -0.2, 0.2), 0.5, 1.5),
        "out_weight": centred(arg_keys[11], (2, DIN, D), DIN ** -0.5, 0.125, ((0, 2), (1, 16))),
    }


epsilon = 1e-05
highest = lax.Precision.HIGHEST

@jax.custom_vjp
def low(v):
    return lax.optimization_barrier(v.astype(jnp.bfloat16)).astype(jnp.float32)

@jax.custom_vjp
def low_back(v):
    return v

def low_keep(v):
    return (low(v), None)

def low_pass(kept, grad):
    return (grad,)

def back_keep(v):
    return (v, None)

def back_low(kept, grad):
    return (low(grad),)
low.defvjp(low_keep, low_pass)
low_back.defvjp(back_keep, back_low)

def norm_rows(values, gain_vec):
    return values * lax.rsqrt(lax.optimization_barrier(jnp.mean(values * values, axis=-1, keepdims=True)) + epsilon) * gain_vec

def causal_conv(signal, kernel, offset):
    taps = kernel.shape[0]
    seq_total = signal.shape[0]
    padded = jnp.pad(signal, ((taps - 1, 0), (0, 0)))
    total = jnp.zeros_like(signal) + offset[None, :]
    for tap_index in range(taps):
        total = total + kernel[tap_index][None, :] * padded[tap_index:tap_index + seq_total]
    return total

def scan_heads(x_heads, dt_heads, decay_rate, b_rows, c_rows, skip_gain):
    seq_total, head_local, head_size = x_heads.shape
    state_width = b_rows.shape[1]
    span_count = seq_total // SPAN
    x_blocks = x_heads.reshape(span_count, SPAN, head_local, head_size)
    b_blocks = b_rows.reshape(span_count, SPAN, state_width)
    c_blocks = c_rows.reshape(span_count, SPAN, state_width)
    dt_blocks = jnp.transpose(dt_heads.reshape(span_count, SPAN, head_local), (0, 2, 1))
    cumulated = jnp.cumsum(dt_blocks * decay_rate[None, :, None], axis=2)
    scores_cb = jnp.einsum('cin,cjn->cij', c_blocks, b_blocks, precision=highest)
    positions = jnp.arange(SPAN)
    lower_mask = (positions[:, None] >= positions[None, :])[None, None]
    diff_decay = cumulated[:, :, :, None] - cumulated[:, :, None, :]
    weighted = jnp.where(lower_mask, jnp.exp(jnp.where(lower_mask, diff_decay, 0.0)), 0.0)
    weighted = weighted * scores_cb[:, None] * dt_blocks[:, :, None, :]
    intra_out = jnp.einsum('chij,cjhp->cihp', weighted, x_blocks, precision=highest)
    last_rate = cumulated[:, :, -1]
    tail_weight = jnp.exp(last_rate[:, :, None] - cumulated) * dt_blocks
    span_states = jnp.einsum('chj,cjn,cjhp->chnp', tail_weight, b_blocks, x_blocks, precision=highest)
    totals_run = jnp.cumsum(last_rate, axis=0)
    start_run = totals_run - last_rate
    span_ids = jnp.arange(span_count)
    before_mask = (span_ids[:, None] > span_ids[None, :])[:, :, None]
    gap_decay = start_run[:, None, :] - totals_run[None, :, :]
    carry_decay = jnp.where(before_mask, jnp.exp(jnp.where(before_mask, gap_decay, 0.0)), 0.0)
    entering = jnp.einsum('ckh,khnp->chnp', carry_decay, span_states, precision=highest)
    inter_out = jnp.einsum('cin,chnp,chi->cihp', c_blocks, entering, jnp.exp(cumulated), precision=highest)
    result = (intra_out + inter_out).reshape(seq_total, head_local, head_size)
    return result + skip_gain[None, :, None] * x_heads

def layer(hidden, length, params):
    norm_gain, in_weight, conv_weight, conv_bias, dt_bias, a_log, d_skip, gated_gain, out_weight = params
    seq_total = hidden.shape[0]
    inner_width = gated_gain.shape[0]
    head_count = dt_bias.shape[0]
    state_width = (conv_weight.shape[1] - inner_width) // 2
    head_size = inner_width // head_count
    head_local = head_count // N_SEQ
    bc_end = 2 * inner_width + 2 * state_width
    valid_rows = (jnp.arange(seq_total) < length).astype(jnp.float32)[:, None]
    normed_in = low(norm_rows(hidden, norm_gain))
    projected = jnp.dot(normed_in, in_weight, precision=highest)
    gate_z = low_back(projected[:, :inner_width])
    conv_in = low(low_back(projected[:, inner_width:bc_end]))
    dt_raw = low(low_back(projected[:, bc_end:]))
    convolved = jax.nn.silu(causal_conv(conv_in, conv_weight, conv_bias))
    x_heads = jnp.transpose(convolved[:, :inner_width].reshape(seq_total, N_SEQ, head_local, head_size), (1, 0, 2, 3))
    b_rows = convolved[:, inner_width:inner_width + state_width]
    c_rows = convolved[:, inner_width + state_width:]
    dt_heads = jnp.transpose(jax.nn.softplus(dt_raw + dt_bias).reshape(seq_total, N_SEQ, head_local), (1, 0, 2))
    decay_rate = (-jnp.exp(a_log)).reshape(N_SEQ, head_local)
    skip_gain = d_skip.reshape(N_SEQ, head_local)

    def one_block(pieces):
        return scan_heads(pieces[0], pieces[1], pieces[2], b_rows, c_rows, pieces[3])
    mixed_heads = lax.map(jax.checkpoint(one_block), (x_heads, dt_heads, decay_rate, skip_gain))
    scanned = low(low_back(jnp.transpose(mixed_heads, (1, 0, 2, 3)).reshape(seq_total, inner_width)))
    gated = scanned * jax.nn.silu(gate_z)
    normed_out = low(norm_rows(gated, gated_gain))
    branch = low_back(jnp.dot(normed_out, out_weight, precision=highest))
    return valid_rows * (hidden + branch)

def reference(inputs, seq_lengths, cotangent, norm_gain, in_weight, conv_weight, conv_bias, dt_bias, a_log, d_skip, gated_gain, out_weight):
    seq_count = MB * N_WSHARD
    start_rows = inputs.astype(jnp.float32).reshape(seq_count, SEQ_LEN, D)
    lengths_flat = seq_lengths.reshape(seq_count)
    weights_all = (norm_gain, in_weight, conv_weight, conv_bias, dt_bias, a_log, d_skip, gated_gain, out_weight)

    def layer_params(layer_index):
        return tuple((weight_arr[layer_index].astype(jnp.float32) for weight_arr in weights_all))

    def run(hidden_all, params):

        def one_seq(pieces):
            return layer(pieces[0], pieces[1], params)
        return lax.map(jax.checkpoint(one_seq), (hidden_all, lengths_flat))
    first_out, pull_first = jax.vjp(run, start_rows, layer_params(0))
    first_act = first_out.astype(jnp.bfloat16)
    second_out, pull_second = jax.vjp(run, first_act.astype(jnp.float32), layer_params(1))
    grad_mid, grads_second = pull_second(cotangent.astype(jnp.float32).reshape(seq_count, SEQ_LEN, D))
    sent_back = grad_mid.astype(jnp.bfloat16)
    grad_start, grads_first = pull_first(sent_back.astype(jnp.float32))
    shape_tok = (MB, N_WSHARD, SEQ_LEN, D)
    acts = jnp.stack([first_act.reshape(shape_tok), second_out.astype(jnp.bfloat16).reshape(shape_tok)])
    grad_in = jnp.stack([grad_start.astype(jnp.bfloat16).reshape(shape_tok), sent_back.reshape(shape_tok)])
    stacked = [jnp.stack([first_grad, second_grad]) for first_grad, second_grad in zip(grads_first, grads_second)]
    return (acts, grad_in, stacked[0], stacked[1], stacked[2], stacked[3], stacked[4], stacked[5], stacked[6], stacked[7], stacked[8])
```

```python
import jax
import jax.numpy as jnp
from jax import lax
from jax.sharding import PartitionSpec as P

LANES = 128
EPSILON = 1e-05
BOTH = ("seq", "wshard")
SWAP = [(0, 1), (1, 0)]
HIGHEST = lax.Precision.HIGHEST


def swapped(array):
    return lax.ppermute(array, "section", SWAP)


def norm_rows(values, gain_vec):
    return (
        values * lax.rsqrt(jnp.mean(values * values, axis=-1, keepdims=True) + EPSILON) * gain_vec
    )


def gate_norm(scanned, gate_z, gain_vec):
    return norm_rows(scanned * jax.nn.silu(gate_z), gain_vec)


def seat_groups(n_seq, micro):
    return [list(range(start, start + micro)) for start in range(0, n_seq, micro)]


def to_sequences(rows, section, micro, n_seq):
    _, t, d = rows.shape
    half = t // 2
    mine = lax.dynamic_slice_in_dim(rows, section * half, half, 1)
    got = lax.all_to_all(
        mine, "seq", 0, 0, axis_index_groups=seat_groups(n_seq, micro), tiled=True
    )
    pairs = got.reshape(2, micro // 2, half, d)
    keep = lax.dynamic_index_in_dim(pairs, section, 0, keepdims=False)
    give = lax.dynamic_index_in_dim(pairs, 1 - section, 0, keepdims=False)
    other = swapped(give)
    first = jnp.where(section == 0, keep, other)
    second = jnp.where(section == 0, other, keep)
    return jnp.stack([first, second], axis=1).reshape(micro * half, d)


def to_pieces(first_rows, second_rows, section, micro, n_seq):
    rows, d = first_rows.shape
    keep = jnp.where(section == 0, first_rows, second_rows)
    give = jnp.where(section == 0, second_rows, first_rows)
    other = swapped(give)
    lo = jnp.where(section == 0, keep, other)
    hi = jnp.where(section == 0, other, keep)
    whole = jnp.concatenate([lo, hi]).reshape(micro, 2 * rows // micro, d)
    return lax.all_to_all(
        whole, "seq", 0, 0, axis_index_groups=seat_groups(n_seq, micro), tiled=True
    )


class Halves:
    def __init__(self, own, other):
        self.own = own
        self.other = other


def fetch(weight, section):
    width = weight.shape[1] // 2
    keep = lax.dynamic_slice_in_dim(weight, section * width, width, 1)
    give = lax.dynamic_slice_in_dim(weight, (1 - section) * width, width, 1)
    got = swapped(give)
    layers = []
    for layer in range(2):
        piece = jnp.where(section == layer, keep, got)
        own = lax.all_gather(piece, BOTH, axis=0, tiled=True)
        layers.append(Halves(own, swapped(own)))
    return layers


def in_order(own, other, section, axis):
    lo = jnp.where(section == 0, own, other)
    hi = jnp.where(section == 0, other, own)
    return jnp.concatenate([lo, hi], axis=axis)


def times(rows, weight, section):
    own = jnp.dot(rows, weight.own, preferred_element_type=jnp.float32)
    other = jnp.dot(rows, weight.other, preferred_element_type=jnp.float32)
    return in_order(own, other, section, 1)


def halves_of(array, section):
    width = array.shape[1] // 2
    return (
        lax.dynamic_slice_in_dim(array, section * width, width, 1),
        lax.dynamic_slice_in_dim(array, (1 - section) * width, width, 1),
    )


def times_back(grad, weight, section):
    own, other = halves_of(grad, section)
    return jnp.einsum(
        "tp,dp->td", own, weight.own, preferred_element_type=jnp.float32
    ) + jnp.einsum("tp,dp->td", other, weight.other, preferred_element_type=jnp.float32)


def bits_of(size):
    return size.bit_length() - 1


def hop_list():
    hops = []
    for axis in BOTH:
        for bit in reversed(range(bits_of(lax.axis_size(axis)))):
            hops.append((axis, 1 << bit))
    return hops


def exchanged(array, axis, distance):
    pairs = [(i, i ^ distance) for i in range(lax.axis_size(axis))]
    return lax.ppermute(array, axis, pairs)


def side_of(axis, distance):
    return (lax.axis_index(axis) // distance) % 2


def add_low(one, two):
    return (one.astype(jnp.float32) + two.astype(jnp.float32)).astype(jnp.bfloat16)


def scatter_sum(array, turned):
    hops = hop_list()
    seat_bits = bits_of(lax.axis_size("seq"))
    order = list(range(seat_bits, len(hops)))
    order = (order if turned else order[::-1]) + list(range(seat_bits))[::-1]
    rows = array.shape[0] >> len(hops)
    array = array.reshape((2,) * len(hops) + (rows, array.shape[1]))
    left = list(range(len(hops)))
    for dim in order:
        axis, distance = hops[dim]
        at = left.index(dim)
        side = side_of(axis, distance)
        give = lax.dynamic_index_in_dim(array, 1 - side, at, keepdims=False)
        keep = lax.dynamic_index_in_dim(array, side, at, keepdims=False)
        array = add_low(keep, exchanged(give, axis, distance))
        left.remove(dim)
    return array


def sum_everywhere(array):
    for axis, distance in hop_list():
        array = array + exchanged(array, axis, distance)
    return array


def weight_sum(rows, grad, section, turned):
    own, other = halves_of(grad, section)
    give = jnp.einsum("td,te->de", rows, other, preferred_element_type=jnp.float32)
    got = swapped(give.astype(jnp.bfloat16))
    keep = jnp.einsum("td,te->de", rows, own, preferred_element_type=jnp.float32)
    return scatter_sum(add_low(keep, got), turned)


def place(first, second, section):
    keep = jnp.where(section == 0, first, second)
    give = jnp.where(section == 0, second, first)
    other = swapped(give)
    return in_order(keep, other, section, 1).astype(jnp.float32)


def mixer(
    conv_in, dt_raw, kernel, offset, dt_offset, a_log, skip, heads, state_width, seat, run, whole_run
):
    tokens = conv_in.shape[0]
    taps = kernel.shape[0]
    inner = conv_in.shape[1] - 2 * state_width
    size = inner // heads
    span = min(256, tokens)
    n_span = tokens // span
    tail = conv_in[tokens - (taps - 1) :]
    halo = before(tail, run, seat, whole_run)
    padded = jnp.concatenate([halo, conv_in], axis=0)
    total = jnp.zeros_like(conv_in) + offset[None, :]
    for tap in range(taps):
        total = total + kernel[tap][None, :] * padded[tap : tap + tokens]
    conv = jax.nn.silu(total)
    x = conv[:, :inner].reshape(n_span, span, heads, size)
    b = conv[:, inner : inner + state_width].reshape(n_span, span, state_width)
    c = conv[:, inner + state_width :].reshape(n_span, span, state_width)
    dt = jax.nn.softplus(dt_raw + dt_offset)
    rate = -jnp.exp(a_log)
    dt_b = jnp.transpose(dt.reshape(n_span, span, heads), (0, 2, 1))
    cum = jnp.cumsum(dt_b * rate[None, :, None], axis=2)
    scores = jnp.einsum("cin,cjn->cij", c, b, precision=HIGHEST)
    ids = jnp.arange(span)
    lower = (ids[:, None] >= ids[None, :])[None, None]
    diff = cum[:, :, :, None] - cum[:, :, None, :]
    weighted = jnp.where(lower, jnp.exp(jnp.where(lower, diff, 0.0)), 0.0)
    weighted = weighted * scores[:, None] * dt_b[:, :, None, :]
    intra = jnp.einsum(
        "chij,cjhp->cihp", weighted.astype(jnp.bfloat16), x.astype(jnp.bfloat16),
        preferred_element_type=jnp.float32,
    )
    last = cum[:, :, -1]
    tail_weight = jnp.exp(last[:, :, None] - cum) * dt_b
    xw = x * jnp.transpose(tail_weight, (0, 2, 1))[..., None]
    states = jnp.einsum(
        "cjn,cjhp->chnp", b.astype(jnp.bfloat16), xw.astype(jnp.bfloat16),
        preferred_element_type=jnp.float32,
    )
    state = jnp.zeros_like(states[0])
    entering = []
    for k in range(n_span):
        entering.append(state)
        state = jnp.exp(last[k])[:, None, None] * state + states[k]
    enter_run = carried(state, jnp.sum(last, axis=0), run, seat, whole_run)
    gone = jnp.zeros_like(last[0])
    shifted = []
    for k in range(n_span):
        shifted.append(entering[k] + jnp.exp(gone)[:, None, None] * enter_run)
        gone = gone + last[k]
    entering = jnp.stack(shifted)
    inter = jnp.einsum(
        "cin,chnp->cihp", c.astype(jnp.bfloat16), entering.astype(jnp.bfloat16),
        preferred_element_type=jnp.float32,
    ) * jnp.transpose(jnp.exp(cum), (0, 2, 1))[..., None]
    out = (intra + inter + skip[None, None, :, None] * x).reshape(tokens, inner)
    return out


def before(tail, run, seat, whole_run):
    n_seq, micro = whole_run
    if n_seq == micro:
        return lax.ppermute(tail, "section", [(0, 1)])
    every = lax.all_gather(tail, ("seq", "section"), axis=0)
    every = every.reshape((n_seq // micro, micro, 2) + tail.shape)
    mine = lax.dynamic_index_in_dim(every, seat % micro, 1, keepdims=False)
    mine = mine.reshape((-1,) + tail.shape)
    past = lax.dynamic_index_in_dim(mine, jnp.maximum(run - 1, 0), 0, keepdims=False)
    return jnp.where(run > 0, past, 0.0)


def carried(state, total, run, seat, whole_run):
    n_seq, micro = whole_run
    if n_seq == micro:
        return lax.ppermute(state.astype(jnp.bfloat16), "section", [(0, 1)]).astype(jnp.float32)
    every = lax.all_gather(state, ("seq", "section"), axis=0)
    totals = lax.all_gather(total, ("seq", "section"), axis=0)
    every = every.reshape((n_seq // micro, micro, 2) + state.shape)
    totals = totals.reshape((n_seq // micro, micro, 2) + total.shape)
    mine = lax.dynamic_index_in_dim(every, seat % micro, 1, keepdims=False)
    mine = mine.reshape((-1,) + state.shape)
    gone = lax.dynamic_index_in_dim(totals, seat % micro, 1, keepdims=False)
    gone = jnp.cumsum(gone.reshape((-1,) + total.shape), axis=0)
    upto = lax.dynamic_index_in_dim(gone, jnp.maximum(run - 1, 0), 0, keepdims=False)
    early = (jnp.arange(mine.shape[0]) < run)[:, None]
    decay = jnp.where(early, jnp.exp(jnp.where(early, upto[None] - gone, 0.0)), 0.0)
    return jnp.einsum("kh,khnp->hnp", decay, mine, precision=HIGHEST)


def local(
    inputs,
    seq_lengths,
    cotangent,
    norm_gain,
    in_weight,
    conv_weight,
    conv_bias,
    dt_bias,
    a_log,
    d_skip,
    gated_gain,
    out_weight,
):
    section = lax.axis_index("section")
    seat = lax.axis_index("seq")
    lane = lax.axis_index("wshard")
    n_seq = lax.axis_size("seq")
    micro, _, piece, width = inputs.shape
    tokens = micro * piece // 2
    inner = gated_gain.shape[1]
    heads = dt_bias.shape[1]
    channels = conv_weight.shape[2]
    state_width = (channels - inner) // 2
    proj = in_weight.shape[2]
    mixed = proj - inner
    padded = -(-mixed // (2 * LANES)) * 2 * LANES
    run = (seat // micro) * 2 + section
    whole_run = (n_seq, micro)

    mix_layers = fetch(
        jnp.pad(in_weight[0, :, inner:], ((0, 0), (0, padded - mixed))), section
    )
    gate_layers = fetch(in_weight[0, :, :inner], section)
    out_layers = fetch(out_weight[0], section)
    hidden_bf = to_sequences(inputs[:, 0], section, micro, n_seq)
    cot = to_sequences(cotangent[:, 0], section, micro, n_seq)

    def both_layers(array):
        other = swapped(array)
        lo = jnp.where(section == 0, array, other)
        hi = jnp.where(section == 0, other, array)
        return (lo[0], hi[0])

    sizes = [norm_gain, conv_weight.reshape(1, -1), conv_bias, dt_bias, a_log, d_skip, gated_gain]
    packed = jnp.concatenate(sizes, axis=1)
    splits = [int(s.shape[1]) for s in sizes]

    def unpack(flat):
        parts, at = [], 0
        for count in splits:
            parts.append(flat[at : at + count])
            at += count
        parts[1] = parts[1].reshape(conv_weight.shape[1:])
        return parts

    params = [unpack(flat) for flat in both_layers(packed)]
    length = lax.dynamic_index_in_dim(
        lax.dynamic_index_in_dim(seq_lengths, seat % micro, 0, keepdims=False), lane, 0,
        keepdims=False,
    )
    positions = run * tokens + jnp.arange(tokens)
    valid = (positions < length).astype(jnp.float32)[:, None]

    kept = []
    layer_outs = []
    for layer in range(2):
        gain_in, kernel, offset, dt_offset, alog, skip, gain_out = params[layer]
        hidden = hidden_bf.astype(jnp.float32)
        normed_in = norm_rows(hidden, gain_in).astype(jnp.bfloat16)
        projected = times(normed_in, mix_layers[layer], section).astype(jnp.bfloat16)
        gate_z = times(normed_in, gate_layers[layer], section)
        conv_in = projected[:, :channels]
        dt_raw = projected[:, channels:mixed]

        def run_mixer(*args):
            return mixer(*args, heads, state_width, seat, run, whole_run)

        mix_args = (
            conv_in.astype(jnp.float32), dt_raw.astype(jnp.float32), kernel, offset, dt_offset,
            alog, skip,
        )
        scanned = run_mixer(*mix_args).astype(jnp.bfloat16)
        normed_out = gate_norm(scanned.astype(jnp.float32), gate_z, gain_out).astype(jnp.bfloat16)
        branch = times(normed_out, out_layers[layer], section)
        layer_out = (valid * (hidden + branch)).astype(jnp.bfloat16)
        kept.append((hidden_bf, normed_in, gate_z, mix_args, run_mixer, scanned, normed_out))
        layer_outs.append(layer_out)
        hidden_bf = layer_out
    acts = to_pieces(layer_outs[0], layer_outs[1], section, micro, n_seq)

    grad_bf = cot
    shard_gate, shard_mix, shard_out = [None] * 2, [None] * 2, [None] * 2
    small, grad_outs = [None] * 2, [None] * 2
    for layer in (1, 0):
        gain_in, kernel, offset, dt_offset, alog, skip, gain_out = params[layer]
        hid, normed_in, gate_z, mix_args, run_mixer, scanned, normed_out = kept[layer]
        masked = grad_bf.astype(jnp.float32) * valid
        grad_branch = masked.astype(jnp.bfloat16)
        shard_out[layer] = weight_sum(normed_out, grad_branch, section, False)
        grad_normed = times_back(grad_branch, out_layers[layer], section)
        _, pull_gate = jax.vjp(gate_norm, scanned.astype(jnp.float32), gate_z, gain_out)
        grad_scanned, grad_gate, grad_gain_out = pull_gate(grad_normed)
        grad_y = grad_scanned.astype(jnp.bfloat16).astype(jnp.float32)
        _, pull_mixer = jax.vjp(run_mixer, *mix_args)
        g_conv, g_dt, g_kernel, g_offset, g_dto, g_alog, g_skip = pull_mixer(grad_y)
        grad_gate = grad_gate.astype(jnp.bfloat16)
        shard_gate[layer] = weight_sum(normed_in, grad_gate, section, True)
        grad_mix = jnp.concatenate(
            [
                g_conv.astype(jnp.bfloat16),
                g_dt.astype(jnp.bfloat16),
                jnp.zeros((tokens, padded - mixed), jnp.bfloat16),
            ],
            axis=1,
        )
        grad_normed_in = times_back(grad_gate, gate_layers[layer], section) + times_back(
            grad_mix, mix_layers[layer], section
        )
        _, pull_norm = jax.vjp(norm_rows, hid.astype(jnp.float32), gain_in)
        grad_hidden, grad_gain_in = pull_norm(grad_normed_in)
        grad_bf = (masked + grad_hidden).astype(jnp.bfloat16)
        shard_mix[layer] = weight_sum(normed_in, grad_mix, section, False)
        grad_outs[layer] = grad_bf
        small[layer] = jnp.concatenate(
            [grad_gain_in, g_kernel.reshape(-1), g_offset, g_dto, g_alog, g_skip, grad_gain_out]
        )
    grads = to_pieces(grad_outs[0], grad_outs[1], section, micro, n_seq)
    mine = jnp.where(section == 0, small[0], small[1])
    others = jnp.where(section == 0, small[1], small[0])
    g = unpack(sum_everywhere(mine + swapped(others)))
    grad_in_weight = jnp.concatenate(
        [
            place(shard_gate[0], shard_gate[1], section),
            place(shard_mix[0], shard_mix[1], section)[:, :mixed],
        ],
        axis=1,
    )
    return (
        acts[None, :, None],
        grads[None, :, None],
        g[0][None],
        grad_in_weight[None],
        g[1][None],
        g[2][None],
        g[3][None],
        g[4][None],
        g[5][None],
        g[6][None],
        place(shard_out[0], shard_out[1], section)[None],
    )


def solution(mesh):
    return jax.shard_map(
        local,
        mesh=mesh,
        in_specs=(
            P(None, "wshard", "seq", None),
            P(),
            P(None, "wshard", "seq", None),
            P("section", None),
            P("section", ("seq", "wshard"), None),
            P("section", None, None),
            P("section", None),
            P("section", None),
            P("section", None),
            P("section", None),
            P("section", None),
            P("section", ("seq", "wshard"), None),
        ),
        out_specs=(
            P("section", None, "wshard", "seq", None),
            P("section", None, "wshard", "seq", None),
            P("section", None),
            P("section", ("seq", "wshard"), None),
            P("section", None, None),
            P("section", None),
            P("section", None),
            P("section", None),
            P("section", None),
            P("section", None),
            P("section", ("seq", "wshard"), None),
        ),
        check_vma=False,
    )
```

```python
import functools

import jax
import jax.numpy as jnp
from jax import lax
from jax.experimental import pallas as pl
from jax.experimental.pallas import tpu as pltpu
from jax.sharding import PartitionSpec as P

LANES = 128
EPSILON = 1e-05
BOTH = ("seq", "wshard")
SWAP = [(0, 1), (1, 0)]
HIGHEST = lax.Precision.HIGHEST


def swapped(array):
    return lax.ppermute(array, "section", SWAP)


def norm_rows(values, gain_vec):
    return (
        values * lax.rsqrt(jnp.mean(values * values, axis=-1, keepdims=True) + EPSILON) * gain_vec
    )


def seat_groups(n_seq, micro):
    return [list(range(start, start + micro)) for start in range(0, n_seq, micro)]


def to_sequences(rows, section, micro, n_seq):
    _, t, d = rows.shape
    half = t // 2
    mine = lax.dynamic_slice_in_dim(rows, section * half, half, 1)
    got = lax.all_to_all(
        mine, "seq", 0, 0, axis_index_groups=seat_groups(n_seq, micro), tiled=True
    )
    pairs = got.reshape(2, micro // 2, half, d)
    keep = lax.dynamic_index_in_dim(pairs, section, 0, keepdims=False)
    give = lax.dynamic_index_in_dim(pairs, 1 - section, 0, keepdims=False)
    other = swapped(give)
    first = jnp.where(section == 0, keep, other)
    second = jnp.where(section == 0, other, keep)
    return jnp.stack([first, second], axis=1).reshape(micro * half, d)


def to_pieces(first_rows, second_rows, section, micro, n_seq):
    rows, d = first_rows.shape
    keep = jnp.where(section == 0, first_rows, second_rows)
    give = jnp.where(section == 0, second_rows, first_rows)
    other = swapped(give)
    lo = jnp.where(section == 0, keep, other)
    hi = jnp.where(section == 0, other, keep)
    whole = jnp.concatenate([lo, hi]).reshape(micro, 2 * rows // micro, d)
    return lax.all_to_all(
        whole, "seq", 0, 0, axis_index_groups=seat_groups(n_seq, micro), tiled=True
    )


class Halves:
    def __init__(self, own, other):
        self.own = own
        self.other = other


def fetch(weight, section):
    width = weight.shape[1] // 2
    keep = lax.dynamic_slice_in_dim(weight, section * width, width, 1)
    give = lax.dynamic_slice_in_dim(weight, (1 - section) * width, width, 1)
    got = swapped(give)
    layers = []
    for layer in range(2):
        piece = jnp.where(section == layer, keep, got)
        own = lax.all_gather(piece, BOTH, axis=0, tiled=True)
        layers.append(Halves(own, swapped(own)))
    return layers


def in_order(own, other, section, axis):
    lo = jnp.where(section == 0, own, other)
    hi = jnp.where(section == 0, other, own)
    return jnp.concatenate([lo, hi], axis=axis)


def times(rows, weight, section, kind):
    own = jnp.dot(rows, weight.own, preferred_element_type=jnp.float32).astype(kind)
    other = jnp.dot(rows, weight.other, preferred_element_type=jnp.float32).astype(kind)
    return in_order(own, other, section, 1)


def halves_of(array, section):
    width = array.shape[1] // 2
    return (
        lax.dynamic_slice_in_dim(array, section * width, width, 1),
        lax.dynamic_slice_in_dim(array, (1 - section) * width, width, 1),
    )


def times_back(grad, weight, section):
    own, other = halves_of(grad, section)
    return jnp.einsum(
        "tp,dp->td", own, weight.own, preferred_element_type=jnp.float32
    ) + jnp.einsum("tp,dp->td", other, weight.other, preferred_element_type=jnp.float32)


def bits_of(size):
    return size.bit_length() - 1


def hop_list():
    hops = []
    for axis in BOTH:
        for bit in reversed(range(bits_of(lax.axis_size(axis)))):
            hops.append((axis, 1 << bit))
    return hops


def exchanged(array, axis, distance):
    pairs = [(i, i ^ distance) for i in range(lax.axis_size(axis))]
    return lax.ppermute(array, axis, pairs)


def side_of(axis, distance):
    return (lax.axis_index(axis) // distance) % 2


def add_low(one, two):
    return (one.astype(jnp.float32) + two.astype(jnp.float32)).astype(jnp.bfloat16)


def scatter_sum(array, turned):
    hops = hop_list()
    seat_bits = bits_of(lax.axis_size("seq"))
    order = list(range(seat_bits, len(hops)))
    order = (order if turned else order[::-1]) + list(range(seat_bits))[::-1]
    rows = array.shape[0] >> len(hops)
    array = array.reshape((2,) * len(hops) + (rows, array.shape[1]))
    left = list(range(len(hops)))
    for dim in order:
        axis, distance = hops[dim]
        at = left.index(dim)
        side = side_of(axis, distance)
        give = lax.dynamic_index_in_dim(array, 1 - side, at, keepdims=False)
        keep = lax.dynamic_index_in_dim(array, side, at, keepdims=False)
        array = add_low(keep, exchanged(give, axis, distance))
        left.remove(dim)
    return array


def sum_everywhere(array):
    for axis, distance in hop_list():
        array = array + exchanged(array, axis, distance)
    return array


def weight_sum(rows, grad, section, turned):
    own, other = halves_of(grad, section)
    give = jnp.einsum("td,te->de", rows, other, preferred_element_type=jnp.float32)
    got = swapped(give.astype(jnp.bfloat16))
    keep = jnp.einsum("td,te->de", rows, own, preferred_element_type=jnp.float32)
    return scatter_sum(add_low(keep, got), turned)


def place(first, second, section):
    keep = jnp.where(section == 0, first, second)
    give = jnp.where(section == 0, second, first)
    other = swapped(give)
    return in_order(keep, other, section, 1).astype(jnp.float32)


BLOCK = 128
LIMIT = 48 * 1024 * 1024
F32 = jnp.float32
BF16 = jnp.bfloat16


def mm(one, two, dims=((1,), (0,)), precision=None):
    return lax.dot_general(
        one, two, (dims, ((), ())), preferred_element_type=F32, precision=precision
    )


def low(value):
    return value.astype(BF16)


def sigmoid(value):
    return 1.0 / (1.0 + jnp.exp(-value))


def triangle(lower, kind):
    rows = lax.broadcasted_iota(jnp.int32, (BLOCK, BLOCK), 0)
    cols = lax.broadcasted_iota(jnp.int32, (BLOCK, BLOCK), 1)
    return jnp.where(rows >= cols if lower else rows <= cols, 1.0, 0.0).astype(kind)


def first_lanes(rows, size):
    return lax.broadcasted_iota(jnp.int32, (rows, LANES), 1) < size


def spread(table, pair, first):
    rows = first.shape[0]
    one = jnp.broadcast_to(table[:, 2 * pair : 2 * pair + 1], (rows, LANES))
    two = jnp.broadcast_to(table[:, 2 * pair + 1 : 2 * pair + 2], (rows, LANES))
    return jnp.where(first, one, two)


def step_sizes(dt_raw, head_ref):
    raw = dt_raw.astype(F32) + head_ref[0:1, :]
    dt = jnp.maximum(raw, 0.0) + jnp.log1p(jnp.exp(-jnp.abs(raw)))
    rate = -jnp.exp(head_ref[1:2, :])
    cum = mm(triangle(True, F32), dt * rate, precision=HIGHEST)
    return raw, dt, rate, cum


def conv_block(xm_ref, prev, taps_ref, at):
    lanes = slice(at, at + LANES)
    whole = jnp.concatenate([prev[8:16, lanes].astype(F32), xm_ref[:, lanes].astype(F32)], axis=0)
    total = jnp.broadcast_to(taps_ref[4:5, lanes], (BLOCK, LANES))
    shifted = []
    for tap in range(4):
        back = 3 - tap
        piece = whole if back == 0 else pltpu.roll(whole, back, 0)
        piece = piece[8:]
        shifted.append(piece)
        total = total + taps_ref[tap : tap + 1, lanes] * piece
    return shifted, total


def states_kernel(
    inner, size, xm_ref, prev_ref, halo_ref, taps_ref, head_ref, conv_ref, enter_ref, out_ref,
    total_ref, state_ref,
):
    step = pl.program_id(0)

    @pl.when(step == 0)
    def _():
        state_ref[...] = jnp.zeros_like(state_ref)
        total_ref[...] = jnp.zeros_like(total_ref)

    prev = jnp.where(step == 0, halo_ref[...].astype(F32), prev_ref[...].astype(F32))
    channels = conv_ref.shape[1]
    for at in range(0, channels, LANES):
        _, total = conv_block(xm_ref, prev, taps_ref, at)
        conv_ref[:, at : at + LANES] = low(total * sigmoid(total))
    _, dt, _, cum = step_sizes(xm_ref[:, channels : channels + LANES], head_ref)
    last = cum[BLOCK - 1 : BLOCK, :]
    tail = jnp.exp(last - cum) * dt
    gone = jnp.exp(last)
    total_ref[...] = total_ref[...] + last
    first = first_lanes(BLOCK, size)
    first_row = first_lanes(1, size)
    b_turned = conv_ref[:, inner : inner + LANES].astype(F32).T.astype(BF16)
    for pair in range(inner // LANES):
        lanes = slice(pair * LANES, (pair + 1) * LANES)
        state = state_ref[:, lanes]
        enter_ref[:, lanes] = low(state)
        weighted = conv_ref[:, lanes].astype(F32) * spread(tail, pair, first)
        state = state * spread(gone, pair, first_row) + mm(b_turned, low(weighted))
        state_ref[:, lanes] = state
        out_ref[:, lanes] = low(state)


def scan_kernel(
    inner, size, conv_ref, raw_ref, enter_ref, into_ref, gate_ref, head_ref, gain_ref, whole_ref,
    y_ref, n_ref, total_ref, gated_ref,
):
    step = pl.program_id(0)

    @pl.when(step == 0)
    def _():
        total_ref[...] = jnp.zeros_like(total_ref)

    _, dt, _, cum = step_sizes(raw_ref[...], head_ref)
    cum_turned = cum.T
    before_block = jnp.exp(total_ref[0:1, :])
    total_ref[...] = total_ref[...] + cum[BLOCK - 1 : BLOCK, :]
    first = first_lanes(BLOCK, size)
    first_row = first_lanes(1, size)
    b = conv_ref[:, inner : inner + LANES]
    c = conv_ref[:, inner + LANES : inner + 2 * LANES]
    scores = mm(c, b, ((1,), (1,))) * triangle(True, F32)
    squares = jnp.zeros((BLOCK, LANES), F32)
    for pair in range(inner // LANES):
        lanes = slice(pair * LANES, (pair + 1) * LANES)
        x = conv_ref[:, lanes].astype(F32)
        entering = low(
            enter_ref[:, lanes].astype(F32)
            + into_ref[:, lanes].astype(F32) * spread(before_block, pair, first_row)
        )
        whole_ref[:, lanes] = entering
        xd = x * spread(dt, pair, first)
        weights = []
        for head in (2 * pair, 2 * pair + 1):
            diff = jnp.minimum(cum[:, head : head + 1] - cum_turned[head : head + 1, :], 0.0)
            weights.append(low(jnp.exp(diff) * scores))
        halves = jnp.concatenate([jnp.where(first, xd, 0.0), jnp.where(first, 0.0, xd)], axis=0)
        y = mm(jnp.concatenate(weights, axis=1), low(halves))
        y = y + mm(c, entering) * jnp.exp(spread(cum, pair, first))
        y = low(y + x * spread(head_ref[2:3, :], pair, first_row))
        y_ref[:, lanes] = y
        z = gate_ref[:, lanes].astype(F32)
        g = y.astype(F32) * z * sigmoid(z)
        gated_ref[:, lanes] = g
        squares = squares + g * g
    scale = lax.rsqrt(jnp.sum(squares, axis=1, keepdims=True) / inner + EPSILON)
    for at in range(0, inner, LANES):
        lanes = slice(at, at + LANES)
        n_ref[:, lanes] = low(gated_ref[:, lanes] * scale * gain_ref[0:1, lanes])


def gate_kernel(
    inner, size, gn_ref, y_ref, gate_ref, c_ref, raw_ref, head_ref, gain_ref, gy_ref, gz_ref,
    gain_sum_ref, into_ref, total_ref, acc_ref,
):
    step = pl.program_id(0)

    @pl.when(step == 0)
    def _():
        total_ref[...] = jnp.zeros_like(total_ref)
        gain_sum_ref[...] = jnp.zeros_like(gain_sum_ref)
        acc_ref[...] = jnp.zeros_like(acc_ref)

    _, _, _, cum = step_sizes(raw_ref[...], head_ref)
    whole = cum + total_ref[0:1, :]
    total_ref[...] = total_ref[...] + cum[BLOCK - 1 : BLOCK, :]
    decay = jnp.exp(whole)
    squares = jnp.zeros((BLOCK, LANES), F32)
    products = jnp.zeros((BLOCK, LANES), F32)
    for at in range(0, inner, LANES):
        lanes = slice(at, at + LANES)
        z = gate_ref[:, lanes].astype(F32)
        g = y_ref[:, lanes].astype(F32) * z * sigmoid(z)
        squares = squares + g * g
        products = products + g * gn_ref[:, lanes].astype(F32) * gain_ref[0:1, lanes]
    scale = lax.rsqrt(jnp.sum(squares, axis=1, keepdims=True) / inner + EPSILON)
    pull = jnp.sum(products, axis=1, keepdims=True) / inner * scale * scale
    c_turned = c_ref[...].astype(F32).T.astype(BF16)
    first = first_lanes(BLOCK, size)
    for pair in range(inner // LANES):
        lanes = slice(pair * LANES, (pair + 1) * LANES)
        z = gate_ref[:, lanes].astype(F32)
        y = y_ref[:, lanes].astype(F32)
        gn = gn_ref[:, lanes].astype(F32)
        sig = sigmoid(z)
        open_z = z * sig
        g = y * open_z
        gain_sum_ref[:, lanes] = gain_sum_ref[:, lanes] + jnp.sum(
            gn * g * scale, axis=0, keepdims=True
        )
        grad = scale * (gn * gain_ref[0:1, lanes] - g * pull)
        gy = low(grad * open_z)
        gy_ref[:, lanes] = gy
        gz_ref[:, lanes] = low(grad * y * sig * (1.0 + z * (1.0 - sig)))
        acc = acc_ref[:, lanes] + mm(c_turned, low(gy.astype(F32) * spread(decay, pair, first)))
        acc_ref[:, lanes] = acc
        into_ref[:, lanes] = low(acc)


def back_kernel(
    inner, size, steps, gy_ref, conv_ref, xm_ref, prev_ref, halo_ref, whole_ref, after_ref,
    taps_ref, head_ref, heads_map_ref, gxm_ref, tap_sum_ref, head_sum_ref, edge_ref, state_ref,
    cum_grad_ref, dt_grad_ref, next_ref,
):
    step = pl.program_id(0)
    channels = conv_ref.shape[1]

    @pl.when(step == 0)
    def _():
        state_ref[...] = after_ref[...].astype(F32)
        tap_sum_ref[...] = jnp.zeros_like(tap_sum_ref)
        head_sum_ref[...] = jnp.zeros_like(head_sum_ref)
        next_ref[...] = jnp.zeros_like(next_ref)

    raw, dt, rate, cum = step_sizes(xm_ref[:, channels : channels + LANES], head_ref)
    cum_turned = cum.T
    last = cum[BLOCK - 1 : BLOCK, :]
    tail = jnp.exp(last - cum)
    gone = jnp.exp(last)
    lower = triangle(True, F32)
    first = first_lanes(BLOCK, size)
    first_row = first_lanes(1, size)
    b = conv_ref[:, inner : inner + LANES]
    c = conv_ref[:, inner + LANES : inner + 2 * LANES]
    c_turned = c.astype(F32).T.astype(BF16)
    scores = mm(c, b, ((1,), (1,))) * lower
    grad_scores = jnp.zeros((BLOCK, BLOCK), F32)
    grad_b = jnp.zeros((BLOCK, LANES), F32)
    grad_c = jnp.zeros((BLOCK, LANES), F32)
    end_rows = []
    skip_rows = []
    prev = jnp.where(step == steps - 1, halo_ref[...].astype(F32), prev_ref[...].astype(F32))

    def conv_back(at, grad_conv):
        lanes = slice(at, at + LANES)
        shifted, total = conv_block(xm_ref, prev, taps_ref, at)
        sig = sigmoid(total)
        g = grad_conv * sig * (1.0 + total * (1.0 - sig))
        rows = [jnp.sum(g * piece, axis=0, keepdims=True) for piece in shifted]
        rows.append(jnp.sum(g, axis=0, keepdims=True))
        rows.append(jnp.zeros((3, LANES), F32))
        tap_sum_ref[:, lanes] = tap_sum_ref[:, lanes] + jnp.concatenate(rows, axis=0)
        long = jnp.concatenate([g, next_ref[:, lanes]], axis=0)
        out = taps_ref[3:4, lanes] * g
        for ahead in (1, 2, 3):
            out = out + taps_ref[3 - ahead : 4 - ahead, lanes] * pltpu.roll(
                long, BLOCK + 8 - ahead, 0
            )[:BLOCK]
        gxm_ref[:, lanes] = low(out)
        next_ref[:, lanes] = g[0:8]

    for pair in range(inner // LANES):
        lanes = slice(pair * LANES, (pair + 1) * LANES)
        x = conv_ref[:, lanes].astype(F32)
        gy_low = gy_ref[:, lanes]
        gy = gy_low.astype(F32)
        dt_here = spread(dt, pair, first)
        cum_here = spread(cum, pair, first)
        tail_here = spread(tail, pair, first)
        xd_low = low(x * dt_here)
        xd = xd_low.astype(F32)
        grad_state = state_ref[:, lanes]
        state_low = low(grad_state)
        entering = whole_ref[:, lanes]
        decays = []
        weights = []
        for head in (2 * pair, 2 * pair + 1):
            diff = jnp.minimum(cum[:, head : head + 1] - cum_turned[head : head + 1, :], 0.0)
            decay = jnp.exp(diff)
            decays.append(decay)
            weights.append(decay * scores)
        xd_halves = low(jnp.concatenate([jnp.where(first, xd, 0.0), jnp.where(first, 0.0, xd)], 0))
        gy_halves = low(jnp.concatenate([jnp.where(first, gy, 0.0), jnp.where(first, 0.0, gy)], 0))
        y = mm(low(jnp.concatenate(weights, axis=1)), xd_halves)
        grad_weights = mm(gy_halves, xd_low, ((1,), (1,)))
        grad_scores = (
            grad_scores + decays[0] * grad_weights[:BLOCK] + decays[1] * grad_weights[BLOCK:]
        )
        turned = low(jnp.concatenate([weights[0].T, weights[1].T], axis=1))
        grad_xd = mm(turned, gy_halves)
        grown = jnp.exp(cum_here)
        y = y + mm(c, entering) * grown
        from_state = mm(b, state_low) * tail_here
        grad_xd = grad_xd + from_state
        gy_grown = low(gy * grown)
        grad_c = grad_c + mm(gy_grown, entering, ((1,), (1,)))
        grad_b = grad_b + mm(low(xd * tail_here), state_low, ((1,), (1,)))
        gone_here = spread(gone, pair, first_row)
        end_rows.append(
            jnp.sum(xd * from_state, axis=0, keepdims=True)
            + gone_here * jnp.sum(entering.astype(F32) * grad_state, axis=0, keepdims=True)
        )
        skip_rows.append(jnp.sum(x * gy, axis=0, keepdims=True))
        state_ref[:, lanes] = grad_state * gone_here + mm(c_turned, gy_grown)
        cum_grad_ref[:, lanes] = gy * y - xd * grad_xd
        dt_grad_ref[:, lanes] = low(x * grad_xd)
        conv_back(pair * LANES, grad_xd * dt_here + gy * spread(head_ref[2:3, :], pair, first_row))
    grad_scores = grad_scores * lower
    grad_c = grad_c + mm(low(grad_scores), b)
    grad_b = grad_b + mm(low(grad_scores.T), c)
    conv_back(inner, grad_b)
    conv_back(inner + LANES, grad_c)
    heads_map = heads_map_ref[...]
    rough = low(cum_grad_ref[...])
    fine = low(cum_grad_ref[...] - rough.astype(F32))
    grad_cum = mm(rough, heads_map) + mm(fine, heads_map)
    rows = jnp.concatenate(
        [jnp.concatenate(end_rows, axis=1), jnp.concatenate(skip_rows, axis=1),
         jnp.zeros((6, inner), F32)], axis=0)
    rows = mm(rows, heads_map.astype(F32), precision=HIGHEST)
    row_ids = lax.broadcasted_iota(jnp.int32, (BLOCK, LANES), 0)
    grad_cum = grad_cum + jnp.where(row_ids == BLOCK - 1, rows[0:1], 0.0)
    grad_log = mm(triangle(False, F32), grad_cum, precision=HIGHEST)
    grad_dt = mm(dt_grad_ref[...], heads_map) + rate * grad_log
    grad_raw = grad_dt * sigmoid(raw)
    gxm_ref[:, channels : channels + LANES] = low(grad_raw)
    if gxm_ref.shape[1] > channels + LANES:
        rest = gxm_ref.shape[1] - channels - LANES
        gxm_ref[:, channels + LANES :] = jnp.zeros((BLOCK, rest), BF16)
    sums = [
        jnp.sum(grad_raw, axis=0, keepdims=True),
        jnp.sum(dt * grad_log, axis=0, keepdims=True) * rate,
        rows[1:2],
        jnp.zeros((5, LANES), F32),
    ]
    head_sum_ref[...] = head_sum_ref[...] + jnp.concatenate(sums, axis=0)

    @pl.when(step == steps - 1)
    def _():
        for at in range(0, channels, LANES):
            lanes = slice(at, at + LANES)
            long = jnp.concatenate([jnp.zeros((8, LANES), F32), next_ref[:, lanes]], axis=0)
            out = jnp.zeros((8, LANES), F32)
            for ahead in (1, 2, 3):
                out = out + taps_ref[3 - ahead : 4 - ahead, lanes] * pltpu.roll(
                    long, 16 - ahead, 0
                )[:8]
            edge_ref[:, lanes] = out


def call(kernel, steps, operands, outs, scratch, flops, turned=False):
    at = (lambda i: steps - 1 - i) if turned else (lambda i: i)

    def spec(block, index):
        return pl.BlockSpec(block, lambda i: index(at(i)))

    moved = sum(a.size * a.dtype.itemsize for a, _, _ in operands)
    return pl.pallas_call(
        kernel,
        grid=(steps,),
        in_specs=[spec(block, index) for _, block, index in operands],
        out_specs=[spec(block, index) for _, _, block, index in outs],
        out_shape=[jax.ShapeDtypeStruct(shape, kind) for shape, kind, _, _ in outs],
        scratch_shapes=[pltpu.VMEM(shape, kind) for shape, kind in scratch],
        compiler_params=pltpu.CompilerParams(
            vmem_limit_bytes=LIMIT, dimension_semantics=("arbitrary",)
        ),
        cost_estimate=pl.CostEstimate(flops=flops, bytes_accessed=moved, transcendentals=0),
    )(*[a for a, _, _ in operands])


def rowwise(i):
    return (i, 0)


def fixed(i):
    return (0, 0)


def run_states(xm, halo, taps, head, inner, size):
    tokens, wide = xm.shape
    channels = taps.shape[1]
    steps = tokens // BLOCK
    per = BLOCK // 16
    return call(
        functools.partial(states_kernel, inner, size),
        steps,
        [
            (xm, (BLOCK, wide), rowwise),
            (xm, (16, wide), lambda i: (jnp.maximum(i * per - 1, 0), 0)),
            (halo, (16, wide), fixed),
            (taps, (8, channels), fixed),
            (head, (8, LANES), fixed),
        ],
        [
            ((tokens, channels), BF16, (BLOCK, channels), rowwise),
            ((steps * LANES, inner), BF16, (LANES, inner), rowwise),
            ((LANES, inner), BF16, (LANES, inner), fixed),
            ((8, LANES), F32, (8, LANES), fixed),
        ],
        [((LANES, inner), F32)],
        2 * tokens * LANES * inner * 4,
    )


def run_scan(conv, xm, enter, into, gate, head, gain, inner, size):
    tokens, channels = conv.shape
    steps = tokens // BLOCK
    at = channels // LANES
    return call(
        functools.partial(scan_kernel, inner, size),
        steps,
        [
            (conv, (BLOCK, channels), rowwise),
            (xm, (BLOCK, LANES), lambda i: (i, at)),
            (enter, (LANES, inner), rowwise),
            (into, (LANES, inner), fixed),
            (gate, (BLOCK, inner), rowwise),
            (head, (8, LANES), fixed),
            (gain, (8, inner), fixed),
        ],
        [
            ((steps * LANES, inner), BF16, (LANES, inner), rowwise),
            ((tokens, inner), BF16, (BLOCK, inner), rowwise),
            ((tokens, inner), BF16, (BLOCK, inner), rowwise),
        ],
        [((8, LANES), F32), ((BLOCK, inner), F32)],
        2 * tokens * LANES * inner * 8,
    )


def run_gate(gn, y, gate, conv, xm, head, gain, inner, size):
    tokens, channels = conv.shape
    steps = tokens // BLOCK
    c_at = channels // LANES - 1
    return call(
        functools.partial(gate_kernel, inner, size),
        steps,
        [
            (gn, (BLOCK, inner), rowwise),
            (y, (BLOCK, inner), rowwise),
            (gate, (BLOCK, inner), rowwise),
            (conv, (BLOCK, LANES), lambda i: (i, c_at)),
            (xm, (BLOCK, LANES), lambda i: (i, c_at + 1)),
            (head, (8, LANES), fixed),
            (gain, (8, inner), fixed),
        ],
        [
            ((tokens, inner), BF16, (BLOCK, inner), rowwise),
            ((tokens, inner), BF16, (BLOCK, inner), rowwise),
            ((8, inner), F32, (8, inner), fixed),
            ((LANES, inner), BF16, (LANES, inner), fixed),
        ],
        [((8, LANES), F32), ((LANES, inner), F32)],
        2 * tokens * LANES * inner * 4,
    )


def run_back(gy, conv, xm, halo, whole, after, taps, head, heads_map, inner, size):
    tokens, channels = conv.shape
    wide = xm.shape[1]
    steps = tokens // BLOCK
    per = BLOCK // 16
    return call(
        functools.partial(back_kernel, inner, size, steps),
        steps,
        [
            (gy, (BLOCK, inner), rowwise),
            (conv, (BLOCK, channels), rowwise),
            (xm, (BLOCK, wide), rowwise),
            (xm, (16, wide), lambda i: (jnp.maximum(i * per - 1, 0), 0)),
            (halo, (16, wide), fixed),
            (whole, (LANES, inner), rowwise),
            (after, (LANES, inner), fixed),
            (taps, (8, channels), fixed),
            (head, (8, LANES), fixed),
            (heads_map, (inner, LANES), fixed),
        ],
        [
            ((tokens, wide), BF16, (BLOCK, wide), rowwise),
            ((8, channels), F32, (8, channels), fixed),
            ((8, LANES), F32, (8, LANES), fixed),
            ((8, channels), F32, (8, channels), fixed),
        ],
        [
            ((LANES, inner), F32),
            ((BLOCK, inner), F32),
            ((BLOCK, inner), BF16),
            ((8, channels), F32),
        ],
        2 * tokens * LANES * inner * 24,
        turned=True,
    )


def of_sequence(array, seat, whole_run):
    n_seq, micro = whole_run
    every = lax.all_gather(array, ("seq", "section"), axis=0)
    every = every.reshape((n_seq // micro, micro, 2) + array.shape)
    mine = lax.dynamic_index_in_dim(every, seat % micro, 1, keepdims=False)
    return mine.reshape((-1,) + array.shape)


def neighbour(array, run, seat, whole_run, by):
    n_seq, micro = whole_run
    if n_seq == micro:
        return lax.ppermute(array, "section", [(0, 1)] if by < 0 else [(1, 0)])
    every = of_sequence(array, seat, whole_run)
    count = every.shape[0]
    found = lax.dynamic_index_in_dim(every, jnp.clip(run + by, 0, count - 1), 0, keepdims=False)
    return jnp.where((run + by >= 0) & (run + by < count), found, 0)


def carried(state, total, run, seat, whole_run, by, size):
    n_seq, micro = whole_run
    if n_seq == micro:
        return neighbour(state, run, seat, whole_run, by)
    states = of_sequence(state, seat, whole_run).astype(jnp.float32)
    totals = of_sequence(total[0], seat, whole_run)
    count = states.shape[0]
    gone = jnp.cumsum(totals, axis=0)
    ids = jnp.arange(count)
    if by < 0:
        edge = lax.dynamic_index_in_dim(gone, jnp.maximum(run - 1, 0), 0, keepdims=False)
        between = edge[None] - gone
        used = (ids < run)[:, None]
    else:
        edge = lax.dynamic_index_in_dim(gone, run, 0, keepdims=False)
        between = gone - totals - edge[None]
        used = (ids > run)[:, None]
    decay = jnp.where(used, jnp.exp(jnp.where(used, between, 0.0)), 0.0)
    heads = state.shape[1] // size
    decay = jnp.repeat(decay[:, :heads], size, axis=1)
    return jnp.sum(decay[:, None, :] * states, axis=0).astype(jnp.bfloat16)


def local(
    inputs,
    seq_lengths,
    cotangent,
    norm_gain,
    in_weight,
    conv_weight,
    conv_bias,
    dt_bias,
    a_log,
    d_skip,
    gated_gain,
    out_weight,
):
    section = lax.axis_index("section")
    seat = lax.axis_index("seq")
    lane = lax.axis_index("wshard")
    n_seq = lax.axis_size("seq")
    micro, _, piece, width = inputs.shape
    tokens = micro * piece // 2
    inner = gated_gain.shape[1]
    heads = dt_bias.shape[1]
    channels = conv_weight.shape[2]
    proj = in_weight.shape[2]
    mixed = proj - inner
    padded = -(-mixed // (2 * LANES)) * 2 * LANES
    run = (seat // micro) * 2 + section
    whole_run = (n_seq, micro)

    mix_layers = fetch(
        jnp.pad(in_weight[0, :, inner:], ((0, 0), (0, padded - mixed))), section
    )
    gate_layers = fetch(in_weight[0, :, :inner], section)
    out_layers = fetch(out_weight[0], section)
    hidden_bf = to_sequences(inputs[:, 0], section, micro, n_seq)
    cot = to_sequences(cotangent[:, 0], section, micro, n_seq)

    def both_layers(array):
        other = swapped(array)
        lo = jnp.where(section == 0, array, other)
        hi = jnp.where(section == 0, other, array)
        return (lo[0], hi[0])

    sizes = [norm_gain, conv_weight.reshape(1, -1), conv_bias, dt_bias, a_log, d_skip, gated_gain]
    packed = jnp.concatenate(sizes, axis=1)
    splits = [int(s.shape[1]) for s in sizes]

    def unpack(flat):
        parts, at = [], 0
        for count in splits:
            parts.append(flat[at : at + count])
            at += count
        parts[1] = parts[1].reshape(conv_weight.shape[1:])
        return parts

    params = [unpack(flat) for flat in both_layers(packed)]
    length = lax.dynamic_index_in_dim(
        lax.dynamic_index_in_dim(seq_lengths, seat % micro, 0, keepdims=False), lane, 0,
        keepdims=False,
    )
    positions = run * tokens + jnp.arange(tokens)
    valid = (positions < length).astype(jnp.float32)[:, None]

    size = inner // heads
    lane_heads = lax.broadcasted_iota(jnp.int32, (inner, LANES), 0) // size
    heads_map = (lane_heads == lax.broadcasted_iota(jnp.int32, (inner, LANES), 1)).astype(
        jnp.bfloat16
    )

    def table(rows, wide):
        rows = [jnp.pad(row, (0, wide - row.shape[0])) for row in rows]
        return jnp.concatenate([jnp.stack(rows), jnp.zeros((8 - len(rows), wide), jnp.float32)])

    tables = []
    for gain_in, kernel, offset, dt_offset, alog, skip, gain_out in params:
        tables.append(
            (
                jnp.concatenate([kernel, offset[None], jnp.zeros((3, channels), jnp.float32)]),
                table([dt_offset, alog, skip], LANES),
                table([gain_out], inner),
            )
        )

    kept = []
    layer_outs = []
    for layer in range(2):
        gain_in = params[layer][0]
        taps, head, gain = tables[layer]
        hidden = hidden_bf.astype(jnp.float32)
        normed_in = norm_rows(hidden, gain_in).astype(jnp.bfloat16)
        xm = times(normed_in, mix_layers[layer], section, jnp.bfloat16)
        gate = times(normed_in, gate_layers[layer], section, jnp.bfloat16)
        halo = neighbour(xm[tokens - 16 :], run, seat, whole_run, -1)
        conv, enter, state, total = run_states(xm, halo, taps, head, inner, size)
        into = carried(state, total, run, seat, whole_run, -1, size)
        whole, y, normed_out = run_scan(conv, xm, enter, into, gate, head, gain, inner, size)
        branch = times(normed_out, out_layers[layer], section, jnp.float32)
        layer_out = (valid * (hidden + branch)).astype(jnp.bfloat16)
        kept.append((hidden_bf, normed_in, gate, xm, halo, conv, total, whole, y, normed_out))
        layer_outs.append(layer_out)
        hidden_bf = layer_out
    acts = to_pieces(layer_outs[0], layer_outs[1], section, micro, n_seq)

    grad_bf = cot
    shard_gate, shard_mix, shard_out = [None] * 2, [None] * 2, [None] * 2
    small, grad_outs = [None] * 2, [None] * 2
    for layer in (1, 0):
        gain_in = params[layer][0]
        taps, head, gain = tables[layer]
        hid, normed_in, gate, xm, halo, conv, total, whole, y, normed_out = kept[layer]
        masked = grad_bf.astype(jnp.float32) * valid
        grad_branch = masked.astype(jnp.bfloat16)
        shard_out[layer] = weight_sum(normed_out, grad_branch, section, False)
        grad_normed = times_back(grad_branch, out_layers[layer], section).astype(jnp.bfloat16)
        grad_y, grad_gate, gain_sum, left = run_gate(
            grad_normed, y, gate, conv, xm, head, gain, inner, size
        )
        after = carried(left, total, run, seat, whole_run, 1, size)
        shard_gate[layer] = weight_sum(normed_in, grad_gate, section, True)
        grad_mix, tap_sum, head_sum, edge = run_back(
            grad_y, conv, xm, halo, whole, after, taps, head, heads_map, inner, size
        )
        edge = neighbour(edge, run, seat, whole_run, 1)
        fixed_rows = grad_mix[tokens - 16 :, :channels].astype(jnp.float32) + jnp.pad(
            edge, ((8, 0), (0, 0))
        )
        grad_mix = lax.dynamic_update_slice(
            grad_mix, fixed_rows.astype(jnp.bfloat16), (tokens - 16, 0)
        )
        grad_normed_in = times_back(grad_gate, gate_layers[layer], section) + times_back(
            grad_mix, mix_layers[layer], section
        )
        _, pull_norm = jax.vjp(norm_rows, hid.astype(jnp.float32), gain_in)
        grad_hidden, grad_gain_in = pull_norm(grad_normed_in)
        grad_bf = (masked + grad_hidden).astype(jnp.bfloat16)
        shard_mix[layer] = weight_sum(normed_in, grad_mix, section, False)
        grad_outs[layer] = grad_bf
        small[layer] = jnp.concatenate(
            [
                grad_gain_in, tap_sum[:4].reshape(-1), tap_sum[4], head_sum[0, :heads],
                head_sum[1, :heads], head_sum[2, :heads], gain_sum[0],
            ]
        )
    grads = to_pieces(grad_outs[0], grad_outs[1], section, micro, n_seq)
    mine = jnp.where(section == 0, small[0], small[1])
    others = jnp.where(section == 0, small[1], small[0])
    g = unpack(sum_everywhere(mine + swapped(others)))
    grad_in_weight = jnp.concatenate(
        [
            place(shard_gate[0], shard_gate[1], section),
            place(shard_mix[0], shard_mix[1], section)[:, :mixed],
        ],
        axis=1,
    )
    return (
        acts[None, :, None],
        grads[None, :, None],
        g[0][None],
        grad_in_weight[None],
        g[1][None],
        g[2][None],
        g[3][None],
        g[4][None],
        g[5][None],
        g[6][None],
        place(shard_out[0], shard_out[1], section)[None],
    )


def solution(mesh):
    return jax.shard_map(
        local,
        mesh=mesh,
        in_specs=(
            P(None, "wshard", "seq", None),
            P(),
            P(None, "wshard", "seq", None),
            P("section", None),
            P("section", ("seq", "wshard"), None),
            P("section", None, None),
            P("section", None),
            P("section", None),
            P("section", None),
            P("section", None),
            P("section", None),
            P("section", ("seq", "wshard"), None),
        ),
        out_specs=(
            P("section", None, "wshard", "seq", None),
            P("section", None, "wshard", "seq", None),
            P("section", None),
            P("section", ("seq", "wshard"), None),
            P("section", None, None),
            P("section", None),
            P("section", None),
            P("section", None),
            P("section", None),
            P("section", None),
            P("section", ("seq", "wshard"), None),
        ),
        check_vma=False,
    )
```

```python
import functools

import jax
import jax.numpy as jnp
from jax import lax
from jax.experimental import pallas as pl
from jax.experimental.pallas import tpu as pltpu
from jax.sharding import PartitionSpec as P

LANES = 128
EPSILON = 1e-05
BOTH = ("seq", "wshard")
SWAP = [(0, 1), (1, 0)]
HIGHEST = lax.Precision.HIGHEST


def swapped(array):
    return lax.ppermute(array, "section", SWAP)


def norm_rows(values, gain_vec):
    return (
        values * lax.rsqrt(jnp.mean(values * values, axis=-1, keepdims=True) + EPSILON) * gain_vec
    )


def seat_groups(n_seq, micro):
    return [list(range(start, start + micro)) for start in range(0, n_seq, micro)]


def to_sequences(rows, section, micro, n_seq, use=()):
    _, t, d = rows.shape
    half = t // 2
    mine = lax.dynamic_slice_in_dim(rows, section * half, half, 1)
    got = lax.all_to_all(
        mine, "seq", 0, 0, axis_index_groups=seat_groups(n_seq, micro), tiled=True
    )
    pairs = later(got, use).reshape(2, micro // 2, half, d)
    keep = lax.dynamic_index_in_dim(pairs, section, 0, keepdims=False)
    give = lax.dynamic_index_in_dim(pairs, 1 - section, 0, keepdims=False)
    other = swapped(give)
    first = jnp.where(section == 0, keep, other)
    second = jnp.where(section == 0, other, keep)
    return jnp.stack([first, second], axis=1).reshape(micro * half, d)


def half_pieces(rows, section, micro):
    count, d = rows.shape
    half = count // micro
    chunks = rows.reshape(micro // 2, 2, half, d)
    keep = lax.dynamic_index_in_dim(chunks, section, 1, keepdims=False)
    give = lax.dynamic_index_in_dim(chunks, 1 - section, 1, keepdims=False)
    other = swapped(give)
    lo = jnp.where(section == 0, keep, other)
    hi = jnp.where(section == 0, other, keep)
    return jnp.concatenate([lo, hi])


def sent_pieces(pieces, micro, n_seq):
    return lax.all_to_all(
        pieces, "seq", 0, 0, axis_index_groups=seat_groups(n_seq, micro), tiled=True
    )


def whole_pieces(first, second, section):
    keep = jnp.where(section == 0, first, second)
    other = swapped(jnp.where(section == 0, second, first))
    lo = jnp.where(section == 0, keep, other)
    hi = jnp.where(section == 0, other, keep)
    return jnp.concatenate([lo, hi], axis=1)


class Halves:
    def __init__(self, own, other):
        self.own = own
        self.other = other


class Gather:
    def __init__(self, array, order):
        self.hops = hop_list()
        self.array = array
        self.order = order

    def step(self, use=(), meet=None):
        if not self.order:
            return meet
        dim = self.order.pop(0)
        axis, distance = self.hops[dim]
        side = side_of(axis, distance)
        got = later(exchanged(self.array, axis, distance), use)
        if meet is not None:
            got, meet = lax.optimization_barrier((got, meet))
        lo = jnp.where(side == 0, self.array, got)
        hi = jnp.where(side == 0, got, self.array)
        self.array = jnp.concatenate([lo, hi], axis=dim)
        return meet

    def part(self, start, end, turned):
        order = self.order[::-1] if turned else list(self.order)
        return Gather(self.array[..., start:end], order)

    def whole(self):
        while self.order:
            self.step()
        return self.array.reshape(-1, self.array.shape[-1])


def by_side(array, rows):
    blocks = array.shape[0] // (2 * rows)
    pair = array.reshape(blocks, 2, rows, array.shape[1])
    return jnp.concatenate([pair[:, 0], pair[:, 1]], axis=2).reshape(
        blocks * rows, 2 * array.shape[1]
    )


def by_rows(array, rows):
    blocks = array.shape[0] // rows
    width = array.shape[1] // 2
    sides = array.reshape(blocks, rows, 2 * width)
    return jnp.stack([sides[..., :width], sides[..., width:]], axis=1).reshape(-1, width)


seen = []


def later(array, others):
    if not len(others):
        return array
    out = lax.optimization_barrier((array,) + tuple(others))
    seen.extend(out[1:])
    return out[0]


def nothing_of(tables):
    total = jnp.zeros((8, LANES), jnp.float32)
    for values in tables:
        total = total + jnp.clip(values[:, :LANES], -1.0, 1.0)
    return total[0] * 0.0


def stage(jobs, *arrays):
    out = lax.optimization_barrier(tuple(arrays_of(jobs)) + arrays)
    for job, array in zip(jobs, out):
        job.array = array
    return out[len(jobs) :]


def arrays_of(jobs):
    return [job.array for job in jobs]


def in_order(own, other, section, axis):
    lo = jnp.where(section == 0, own, other)
    hi = jnp.where(section == 0, other, own)
    return jnp.concatenate([lo, hi], axis=axis)


def times(rows, weight, section, kind):
    own = jnp.dot(rows, weight.own, preferred_element_type=jnp.float32).astype(kind)
    other = jnp.dot(rows, weight.other, preferred_element_type=jnp.float32).astype(kind)
    return in_order(own, other, section, 1)


def halves_of(array, section):
    width = array.shape[1] // 2
    return (
        lax.dynamic_slice_in_dim(array, section * width, width, 1),
        lax.dynamic_slice_in_dim(array, (1 - section) * width, width, 1),
    )


def times_back(grad, weight, section):
    own, other = halves_of(grad, section)
    return jnp.einsum(
        "tp,dp->td", own, weight.own, preferred_element_type=jnp.float32
    ) + jnp.einsum("tp,dp->td", other, weight.other, preferred_element_type=jnp.float32)


def bits_of(size):
    return size.bit_length() - 1


def hop_list():
    hops = []
    for axis in BOTH:
        for bit in reversed(range(bits_of(lax.axis_size(axis)))):
            hops.append((axis, 1 << bit))
    return hops


def exchanged(array, axis, distance):
    pairs = [(i, i ^ distance) for i in range(lax.axis_size(axis))]
    return lax.ppermute(array, axis, pairs)


def side_of(axis, distance):
    return (lax.axis_index(axis) // distance) % 2


def add_low(one, two):
    return (one.astype(jnp.float32) + two.astype(jnp.float32)).astype(jnp.bfloat16)


class Scatter:
    def __init__(self, array, turned):
        hops = hop_list()
        seat_bits = bits_of(lax.axis_size("seq"))
        order = list(range(seat_bits, len(hops)))
        self.order = (order if turned else order[::-1]) + list(range(seat_bits))[::-1]
        self.hops = hops
        self.left = list(range(len(hops)))
        self.array = array.reshape(
            (2,) * len(hops) + (array.shape[0] >> len(hops), array.shape[1])
        )

    def step(self, start=(), use=()):
        if not self.order:
            return
        dim = self.order.pop(0)
        axis, distance = self.hops[dim]
        at = self.left.index(dim)
        side = side_of(axis, distance)
        array = later(self.array, start)
        give = lax.dynamic_index_in_dim(array, 1 - side, at, keepdims=False)
        keep = lax.dynamic_index_in_dim(array, side, at, keepdims=False)
        self.array = add_low(keep, later(exchanged(give, axis, distance), use))
        self.left.remove(dim)

    def joined(self, other):
        out = Scatter.__new__(Scatter)
        out.hops, out.left, out.order = self.hops, self.left, self.order
        out.array = jnp.concatenate([self.array, other.array], axis=-1)
        return out

    def shard(self):
        while self.order:
            self.step()
        return self.array


def weight_sum(rows, grad, section):
    own, other = halves_of(grad, section)
    give = jnp.einsum("td,te->de", rows, other, preferred_element_type=jnp.float32)
    got = swapped(give.astype(jnp.bfloat16))
    keep = jnp.einsum("td,te->de", rows, own, preferred_element_type=jnp.float32)
    return add_low(keep, got)


BLOCK = 128
LIMIT = 48 * 1024 * 1024
F32 = jnp.float32
BF16 = jnp.bfloat16


def mm(one, two, dims=((1,), (0,)), precision=None):
    return lax.dot_general(
        one, two, (dims, ((), ())), preferred_element_type=F32, precision=precision
    )


def low(value):
    return value.astype(BF16)


def sigmoid(value):
    return 1.0 / (1.0 + jnp.exp(-value))


def triangle(lower, kind):
    rows = lax.broadcasted_iota(jnp.int32, (BLOCK, BLOCK), 0)
    cols = lax.broadcasted_iota(jnp.int32, (BLOCK, BLOCK), 1)
    return jnp.where(rows >= cols if lower else rows <= cols, 1.0, 0.0).astype(kind)


def first_lanes(rows, size):
    return lax.broadcasted_iota(jnp.int32, (rows, LANES), 1) < size


def spread(table, pair, first):
    rows = first.shape[0]
    one = jnp.broadcast_to(table[:, 2 * pair : 2 * pair + 1], (rows, LANES))
    two = jnp.broadcast_to(table[:, 2 * pair + 1 : 2 * pair + 2], (rows, LANES))
    return jnp.where(first, one, two)


def step_sizes(dt_raw, head_ref):
    raw = dt_raw.astype(F32) + head_ref[0:1, :]
    dt = jnp.maximum(raw, 0.0) + jnp.log1p(jnp.exp(-jnp.abs(raw)))
    rate = -jnp.exp(head_ref[1:2, :])
    cum = mm(triangle(True, F32), dt * rate, precision=HIGHEST)
    return raw, dt, rate, cum


def conv_block(xm_ref, prev, taps_ref, at):
    lanes = slice(at, at + LANES)
    whole = jnp.concatenate([prev[8:16, lanes].astype(F32), xm_ref[:, lanes].astype(F32)], axis=0)
    total = jnp.broadcast_to(taps_ref[4:5, lanes], (BLOCK, LANES))
    shifted = []
    for tap in range(4):
        back = 3 - tap
        piece = whole if back == 0 else pltpu.roll(whole, back, 0)
        piece = piece[8:]
        shifted.append(piece)
        total = total + taps_ref[tap : tap + 1, lanes] * piece
    return shifted, total


def states_kernel(
    inner, size, xm_ref, prev_ref, halo_ref, taps_ref, head_ref, conv_ref, enter_ref, out_ref,
    total_ref, state_ref,
):
    step = pl.program_id(0)

    @pl.when(step == 0)
    def _():
        state_ref[...] = jnp.zeros_like(state_ref)
        total_ref[...] = jnp.zeros_like(total_ref)

    prev = jnp.where(step == 0, halo_ref[...].astype(F32), prev_ref[...].astype(F32))
    channels = conv_ref.shape[1]
    for at in range(0, channels, LANES):
        _, total = conv_block(xm_ref, prev, taps_ref, at)
        conv_ref[:, at : at + LANES] = low(total * sigmoid(total))
    _, dt, _, cum = step_sizes(xm_ref[:, channels : channels + LANES], head_ref)
    last = cum[BLOCK - 1 : BLOCK, :]
    tail = jnp.exp(last - cum) * dt
    gone = jnp.exp(last)
    total_ref[...] = total_ref[...] + last
    first = first_lanes(BLOCK, size)
    first_row = first_lanes(1, size)
    b_turned = conv_ref[:, inner : inner + LANES].astype(F32).T.astype(BF16)
    for pair in range(inner // LANES):
        lanes = slice(pair * LANES, (pair + 1) * LANES)
        state = state_ref[:, lanes]
        enter_ref[:, lanes] = low(state)
        weighted = conv_ref[:, lanes].astype(F32) * spread(tail, pair, first)
        state = state * spread(gone, pair, first_row) + mm(b_turned, low(weighted))
        state_ref[:, lanes] = state
        out_ref[:, lanes] = low(state)


def scan_kernel(
    inner, size, conv_ref, raw_ref, enter_ref, into_ref, gate_ref, head_ref, gain_ref, whole_ref,
    y_ref, n_ref, total_ref, gated_ref,
):
    step = pl.program_id(0)

    @pl.when(step == 0)
    def _():
        total_ref[...] = jnp.zeros_like(total_ref)

    _, dt, _, cum = step_sizes(raw_ref[...], head_ref)
    cum_turned = cum.T
    before_block = jnp.exp(total_ref[0:1, :])
    total_ref[...] = total_ref[...] + cum[BLOCK - 1 : BLOCK, :]
    first = first_lanes(BLOCK, size)
    first_row = first_lanes(1, size)
    b = conv_ref[:, inner : inner + LANES]
    c = conv_ref[:, inner + LANES : inner + 2 * LANES]
    scores = mm(c, b, ((1,), (1,))) * triangle(True, F32)
    squares = jnp.zeros((BLOCK, LANES), F32)
    for pair in range(inner // LANES):
        lanes = slice(pair * LANES, (pair + 1) * LANES)
        x = conv_ref[:, lanes].astype(F32)
        entering = low(
            enter_ref[:, lanes].astype(F32)
            + into_ref[:, lanes].astype(F32) * spread(before_block, pair, first_row)
        )
        whole_ref[:, lanes] = entering
        xd = x * spread(dt, pair, first)
        weights = []
        for head in (2 * pair, 2 * pair + 1):
            diff = jnp.minimum(cum[:, head : head + 1] - cum_turned[head : head + 1, :], 0.0)
            weights.append(low(jnp.exp(diff) * scores))
        halves = jnp.concatenate([jnp.where(first, xd, 0.0), jnp.where(first, 0.0, xd)], axis=0)
        y = mm(jnp.concatenate(weights, axis=1), low(halves))
        y = y + mm(c, entering) * jnp.exp(spread(cum, pair, first))
        y = low(y + x * spread(head_ref[2:3, :], pair, first_row))
        y_ref[:, lanes] = y
        z = gate_ref[:, lanes].astype(F32)
        g = y.astype(F32) * z * sigmoid(z)
        gated_ref[:, lanes] = g
        squares = squares + g * g
    scale = lax.rsqrt(jnp.sum(squares, axis=1, keepdims=True) / inner + EPSILON)
    for at in range(0, inner, LANES):
        lanes = slice(at, at + LANES)
        n_ref[:, lanes] = low(gated_ref[:, lanes] * scale * gain_ref[0:1, lanes])


def gate_kernel(
    inner, size, gn_ref, y_ref, gate_ref, c_ref, raw_ref, head_ref, gain_ref, gy_ref, gz_ref,
    gain_sum_ref, into_ref, total_ref, acc_ref,
):
    step = pl.program_id(0)

    @pl.when(step == 0)
    def _():
        total_ref[...] = jnp.zeros_like(total_ref)
        gain_sum_ref[...] = jnp.zeros_like(gain_sum_ref)
        acc_ref[...] = jnp.zeros_like(acc_ref)

    _, _, _, cum = step_sizes(raw_ref[...], head_ref)
    whole = cum + total_ref[0:1, :]
    total_ref[...] = total_ref[...] + cum[BLOCK - 1 : BLOCK, :]
    decay = jnp.exp(whole)
    squares = jnp.zeros((BLOCK, LANES), F32)
    products = jnp.zeros((BLOCK, LANES), F32)
    for at in range(0, inner, LANES):
        lanes = slice(at, at + LANES)
        z = gate_ref[:, lanes].astype(F32)
        g = y_ref[:, lanes].astype(F32) * z * sigmoid(z)
        squares = squares + g * g
        products = products + g * gn_ref[:, lanes].astype(F32) * gain_ref[0:1, lanes]
    scale = lax.rsqrt(jnp.sum(squares, axis=1, keepdims=True) / inner + EPSILON)
    pull = jnp.sum(products, axis=1, keepdims=True) / inner * scale * scale
    c_turned = c_ref[...].astype(F32).T.astype(BF16)
    first = first_lanes(BLOCK, size)
    for pair in range(inner // LANES):
        lanes = slice(pair * LANES, (pair + 1) * LANES)
        z = gate_ref[:, lanes].astype(F32)
        y = y_ref[:, lanes].astype(F32)
        gn = gn_ref[:, lanes].astype(F32)
        sig = sigmoid(z)
        open_z = z * sig
        g = y * open_z
        gain_sum_ref[:, lanes] = gain_sum_ref[:, lanes] + jnp.sum(
            gn * g * scale, axis=0, keepdims=True
        )
        grad = scale * (gn * gain_ref[0:1, lanes] - g * pull)
        gy = low(grad * open_z)
        gy_ref[:, lanes] = gy
        gz_ref[:, lanes] = low(grad * y * sig * (1.0 + z * (1.0 - sig)))
        acc = acc_ref[:, lanes] + mm(c_turned, low(gy.astype(F32) * spread(decay, pair, first)))
        acc_ref[:, lanes] = acc
        into_ref[:, lanes] = low(acc)


def back_kernel(
    inner, size, steps, gy_ref, conv_ref, xm_ref, prev_ref, halo_ref, whole_ref, after_ref,
    taps_ref, head_ref, heads_map_ref, gxm_ref, tap_sum_ref, head_sum_ref, edge_ref, state_ref,
    cum_grad_ref, dt_grad_ref, next_ref,
):
    step = pl.program_id(0)
    channels = conv_ref.shape[1]

    @pl.when(step == 0)
    def _():
        state_ref[...] = after_ref[...].astype(F32)
        tap_sum_ref[...] = jnp.zeros_like(tap_sum_ref)
        head_sum_ref[...] = jnp.zeros_like(head_sum_ref)
        next_ref[...] = jnp.zeros_like(next_ref)

    raw, dt, rate, cum = step_sizes(xm_ref[:, channels : channels + LANES], head_ref)
    cum_turned = cum.T
    last = cum[BLOCK - 1 : BLOCK, :]
    tail = jnp.exp(last - cum)
    gone = jnp.exp(last)
    lower = triangle(True, F32)
    first = first_lanes(BLOCK, size)
    first_row = first_lanes(1, size)
    b = conv_ref[:, inner : inner + LANES]
    c = conv_ref[:, inner + LANES : inner + 2 * LANES]
    c_turned = c.astype(F32).T.astype(BF16)
    scores = mm(c, b, ((1,), (1,))) * lower
    grad_scores = jnp.zeros((BLOCK, BLOCK), F32)
    grad_b = jnp.zeros((BLOCK, LANES), F32)
    grad_c = jnp.zeros((BLOCK, LANES), F32)
    end_rows = []
    skip_rows = []
    prev = jnp.where(step == steps - 1, halo_ref[...].astype(F32), prev_ref[...].astype(F32))

    def conv_back(at, grad_conv):
        lanes = slice(at, at + LANES)
        shifted, total = conv_block(xm_ref, prev, taps_ref, at)
        sig = sigmoid(total)
        g = grad_conv * sig * (1.0 + total * (1.0 - sig))
        rows = [jnp.sum(g * piece, axis=0, keepdims=True) for piece in shifted]
        rows.append(jnp.sum(g, axis=0, keepdims=True))
        rows.append(jnp.zeros((3, LANES), F32))
        tap_sum_ref[:, lanes] = tap_sum_ref[:, lanes] + jnp.concatenate(rows, axis=0)
        long = jnp.concatenate([g, next_ref[:, lanes]], axis=0)
        out = taps_ref[3:4, lanes] * g
        for ahead in (1, 2, 3):
            out = out + taps_ref[3 - ahead : 4 - ahead, lanes] * pltpu.roll(
                long, BLOCK + 8 - ahead, 0
            )[:BLOCK]
        gxm_ref[:, lanes] = low(out)
        next_ref[:, lanes] = g[0:8]

    for pair in range(inner // LANES):
        lanes = slice(pair * LANES, (pair + 1) * LANES)
        x = conv_ref[:, lanes].astype(F32)
        gy_low = gy_ref[:, lanes]
        gy = gy_low.astype(F32)
        dt_here = spread(dt, pair, first)
        cum_here = spread(cum, pair, first)
        tail_here = spread(tail, pair, first)
        xd_low = low(x * dt_here)
        xd = xd_low.astype(F32)
        grad_state = state_ref[:, lanes]
        state_low = low(grad_state)
        entering = whole_ref[:, lanes]
        decays = []
        weights = []
        for head in (2 * pair, 2 * pair + 1):
            diff = jnp.minimum(cum[:, head : head + 1] - cum_turned[head : head + 1, :], 0.0)
            decay = jnp.exp(diff)
            decays.append(decay)
            weights.append(decay * scores)
        xd_halves = low(jnp.concatenate([jnp.where(first, xd, 0.0), jnp.where(first, 0.0, xd)], 0))
        gy_halves = low(jnp.concatenate([jnp.where(first, gy, 0.0), jnp.where(first, 0.0, gy)], 0))
        y = mm(low(jnp.concatenate(weights, axis=1)), xd_halves)
        grad_weights = mm(gy_halves, xd_low, ((1,), (1,)))
        grad_scores = (
            grad_scores + decays[0] * grad_weights[:BLOCK] + decays[1] * grad_weights[BLOCK:]
        )
        turned = low(jnp.concatenate([weights[0].T, weights[1].T], axis=1))
        grad_xd = mm(turned, gy_halves)
        grown = jnp.exp(cum_here)
        y = y + mm(c, entering) * grown
        from_state = mm(b, state_low) * tail_here
        grad_xd = grad_xd + from_state
        gy_grown = low(gy * grown)
        grad_c = grad_c + mm(gy_grown, entering, ((1,), (1,)))
        grad_b = grad_b + mm(low(xd * tail_here), state_low, ((1,), (1,)))
        gone_here = spread(gone, pair, first_row)
        end_rows.append(
            jnp.sum(xd * from_state, axis=0, keepdims=True)
            + gone_here * jnp.sum(entering.astype(F32) * grad_state, axis=0, keepdims=True)
        )
        skip_rows.append(jnp.sum(x * gy, axis=0, keepdims=True))
        state_ref[:, lanes] = grad_state * gone_here + mm(c_turned, gy_grown)
        cum_grad_ref[:, lanes] = gy * y - xd * grad_xd
        dt_grad_ref[:, lanes] = low(x * grad_xd)
        conv_back(pair * LANES, grad_xd * dt_here + gy * spread(head_ref[2:3, :], pair, first_row))
    grad_scores = grad_scores * lower
    grad_c = grad_c + mm(low(grad_scores), b)
    grad_b = grad_b + mm(low(grad_scores.T), c)
    conv_back(inner, grad_b)
    conv_back(inner + LANES, grad_c)
    heads_map = heads_map_ref[...]
    rough = low(cum_grad_ref[...])
    fine = low(cum_grad_ref[...] - rough.astype(F32))
    grad_cum = mm(rough, heads_map) + mm(fine, heads_map)
    rows = jnp.concatenate(
        [jnp.concatenate(end_rows, axis=1), jnp.concatenate(skip_rows, axis=1),
         jnp.zeros((6, inner), F32)], axis=0)
    rows = mm(rows, heads_map.astype(F32), precision=HIGHEST)
    row_ids = lax.broadcasted_iota(jnp.int32, (BLOCK, LANES), 0)
    grad_cum = grad_cum + jnp.where(row_ids == BLOCK - 1, rows[0:1], 0.0)
    grad_log = mm(triangle(False, F32), grad_cum, precision=HIGHEST)
    grad_dt = mm(dt_grad_ref[...], heads_map) + rate * grad_log
    grad_raw = grad_dt * sigmoid(raw)
    gxm_ref[:, channels : channels + LANES] = low(grad_raw)
    if gxm_ref.shape[1] > channels + LANES:
        rest = gxm_ref.shape[1] - channels - LANES
        gxm_ref[:, channels + LANES :] = jnp.zeros((BLOCK, rest), BF16)
    sums = [
        jnp.sum(grad_raw, axis=0, keepdims=True),
        jnp.sum(dt * grad_log, axis=0, keepdims=True) * rate,
        rows[1:2],
        jnp.zeros((5, LANES), F32),
    ]
    head_sum_ref[...] = head_sum_ref[...] + jnp.concatenate(sums, axis=0)

    @pl.when(step == steps - 1)
    def _():
        for at in range(0, channels, LANES):
            lanes = slice(at, at + LANES)
            long = jnp.concatenate([jnp.zeros((8, LANES), F32), next_ref[:, lanes]], axis=0)
            out = jnp.zeros((8, LANES), F32)
            for ahead in (1, 2, 3):
                out = out + taps_ref[3 - ahead : 4 - ahead, lanes] * pltpu.roll(
                    long, 16 - ahead, 0
                )[:8]
            edge_ref[:, lanes] = out


def call(kernel, steps, operands, outs, scratch, flops, waits, turned=False):
    count = len(operands)

    def body(*refs):
        kernel(*refs[:count], *refs[count + len(waits) :])

    at = (lambda i: steps - 1 - i) if turned else (lambda i: i)

    def spec(block, index):
        return pl.BlockSpec(block, lambda i: index(at(i)))

    moved = sum(a.size * a.dtype.itemsize for a, _, _ in operands) // 8
    return pl.pallas_call(
        body,
        grid=(steps,),
        in_specs=[spec(block, index) for _, block, index in operands]
        + [pl.BlockSpec(memory_space=pl.ANY)] * len(waits),
        out_specs=[spec(block, index) for _, _, block, index in outs],
        out_shape=[jax.ShapeDtypeStruct(shape, kind) for shape, kind, _, _ in outs],
        scratch_shapes=[pltpu.VMEM(shape, kind) for shape, kind in scratch],
        compiler_params=pltpu.CompilerParams(
            vmem_limit_bytes=LIMIT, dimension_semantics=("arbitrary",)
        ),
        cost_estimate=pl.CostEstimate(flops=flops, bytes_accessed=moved, transcendentals=0),
    )(*[a for a, _, _ in operands], *waits)


def rowwise(i):
    return (i, 0)


def fixed(i):
    return (0, 0)


def run_states(xm, halo, taps, head, inner, size, waits=()):
    tokens, wide = xm.shape
    channels = taps.shape[1]
    steps = tokens // BLOCK
    per = BLOCK // 16
    return call(
        functools.partial(states_kernel, inner, size),
        steps,
        [
            (xm, (BLOCK, wide), rowwise),
            (xm, (16, wide), lambda i: (jnp.maximum(i * per - 1, 0), 0)),
            (halo, (16, wide), fixed),
            (taps, (8, channels), fixed),
            (head, (8, LANES), fixed),
        ],
        [
            ((tokens, channels), BF16, (BLOCK, channels), rowwise),
            ((steps * LANES, inner), BF16, (LANES, inner), rowwise),
            ((LANES, inner), BF16, (LANES, inner), fixed),
            ((8, LANES), F32, (8, LANES), fixed),
        ],
        [((LANES, inner), F32)],
        tokens * inner * 900,
        waits,
    )


def run_scan(conv, xm, enter, into, gate, head, gain, inner, size, waits=()):
    tokens, channels = conv.shape
    steps = tokens // BLOCK
    at = channels // LANES
    return call(
        functools.partial(scan_kernel, inner, size),
        steps,
        [
            (conv, (BLOCK, channels), rowwise),
            (xm, (BLOCK, LANES), lambda i: (i, at)),
            (enter, (LANES, inner), rowwise),
            (into, (LANES, inner), fixed),
            (gate, (BLOCK, inner), rowwise),
            (head, (8, LANES), fixed),
            (gain, (8, inner), fixed),
        ],
        [
            ((steps * LANES, inner), BF16, (LANES, inner), rowwise),
            ((tokens, inner), BF16, (BLOCK, inner), rowwise),
            ((tokens, inner), BF16, (BLOCK, inner), rowwise),
            ((8, LANES), F32, (8, LANES), fixed),
        ],
        [((BLOCK, inner), F32)],
        tokens * inner * 1100,
        waits,
    )


def run_gate(gn, y, gate, conv, xm, head, gain, inner, size, waits=()):
    tokens, channels = conv.shape
    steps = tokens // BLOCK
    c_at = channels // LANES - 1
    return call(
        functools.partial(gate_kernel, inner, size),
        steps,
        [
            (gn, (BLOCK, inner), rowwise),
            (y, (BLOCK, inner), rowwise),
            (gate, (BLOCK, inner), rowwise),
            (conv, (BLOCK, LANES), lambda i: (i, c_at)),
            (xm, (BLOCK, LANES), lambda i: (i, c_at + 1)),
            (head, (8, LANES), fixed),
            (gain, (8, inner), fixed),
        ],
        [
            ((tokens, inner), BF16, (BLOCK, inner), rowwise),
            ((tokens, inner), BF16, (BLOCK, inner), rowwise),
            ((8, inner), F32, (8, inner), fixed),
            ((LANES, inner), BF16, (LANES, inner), fixed),
        ],
        [((8, LANES), F32), ((LANES, inner), F32)],
        tokens * inner * 1000,
        waits,
    )


def run_back(gy, conv, xm, halo, whole, after, taps, head, heads_map, inner, size, waits=()):
    tokens, channels = conv.shape
    wide = xm.shape[1]
    steps = tokens // BLOCK
    per = BLOCK // 16
    return call(
        functools.partial(back_kernel, inner, size, steps),
        steps,
        [
            (gy, (BLOCK, inner), rowwise),
            (conv, (BLOCK, channels), rowwise),
            (xm, (BLOCK, wide), rowwise),
            (xm, (16, wide), lambda i: (jnp.maximum(i * per - 1, 0), 0)),
            (halo, (16, wide), fixed),
            (whole, (LANES, inner), rowwise),
            (after, (LANES, inner), fixed),
            (taps, (8, channels), fixed),
            (head, (8, LANES), fixed),
            (heads_map, (inner, LANES), fixed),
        ],
        [
            ((tokens, wide), BF16, (BLOCK, wide), rowwise),
            ((8, channels), F32, (8, channels), fixed),
            ((8, LANES), F32, (8, LANES), fixed),
            ((8, channels), F32, (8, channels), fixed),
        ],
        [
            ((LANES, inner), F32),
            ((BLOCK, inner), F32),
            ((BLOCK, inner), BF16),
            ((8, channels), F32),
        ],
        tokens * inner * 3000,
        waits,
        turned=True,
    )


def of_sequence(array, seat, whole_run):
    n_seq, micro = whole_run
    every = lax.all_gather(array, ("seq", "section"), axis=0)
    every = every.reshape((n_seq // micro, micro, 2) + array.shape)
    mine = lax.dynamic_index_in_dim(every, seat % micro, 1, keepdims=False)
    return mine.reshape((-1,) + array.shape)


def neighbour(array, run, seat, whole_run, by):
    n_seq, micro = whole_run
    if n_seq == micro:
        return lax.ppermute(array, "section", [(0, 1)] if by < 0 else [(1, 0)])
    every = of_sequence(array, seat, whole_run)
    count = every.shape[0]
    found = lax.dynamic_index_in_dim(every, jnp.clip(run + by, 0, count - 1), 0, keepdims=False)
    return jnp.where((run + by >= 0) & (run + by < count), found, 0)


def carried(state, total, run, seat, whole_run, by, size):
    n_seq, micro = whole_run
    if n_seq == micro:
        return neighbour(state, run, seat, whole_run, by)
    states = of_sequence(state, seat, whole_run).astype(jnp.float32)
    totals = of_sequence(total[0], seat, whole_run)
    count = states.shape[0]
    gone = jnp.cumsum(totals, axis=0)
    ids = jnp.arange(count)
    if by < 0:
        edge = lax.dynamic_index_in_dim(gone, jnp.maximum(run - 1, 0), 0, keepdims=False)
        between = edge[None] - gone
        used = (ids < run)[:, None]
    else:
        edge = lax.dynamic_index_in_dim(gone, run, 0, keepdims=False)
        between = gone - totals - edge[None]
        used = (ids > run)[:, None]
    decay = jnp.where(used, jnp.exp(jnp.where(used, between, 0.0)), 0.0)
    heads = state.shape[1] // size
    decay = jnp.repeat(decay[:, :heads], size, axis=1)
    return jnp.sum(decay[:, None, :] * states, axis=0).astype(jnp.bfloat16)


def local(
    inputs,
    seq_lengths,
    cotangent,
    norm_gain,
    in_weight,
    conv_weight,
    conv_bias,
    dt_bias,
    a_log,
    d_skip,
    gated_gain,
    out_weight,
):
    seen.clear()
    section = lax.axis_index("section")
    seat = lax.axis_index("seq")
    lane = lax.axis_index("wshard")
    n_seq = lax.axis_size("seq")
    micro, _, piece, width = inputs.shape
    tokens = micro * piece // 2
    inner = gated_gain.shape[1]
    heads = dt_bias.shape[1]
    channels = conv_weight.shape[2]
    proj = in_weight.shape[2]
    mixed = proj - inner
    padded = -(-mixed // (2 * LANES)) * 2 * LANES
    run = (seat // micro) * 2 + section
    whole_run = (n_seq, micro)

    rows_in = in_weight.shape[1]
    mix_shard = jnp.pad(in_weight[0, :, inner:], ((0, 0), (0, padded - mixed)))
    gate_shard = in_weight[0, :, :inner]
    mix_half, gate_half = padded // 2, inner // 2
    out_half = out_weight.shape[2] // 2

    def packed(side):
        return jnp.concatenate(
            [
                mix_shard[:, side * mix_half : (side + 1) * mix_half],
                gate_shard[:, side * gate_half : (side + 1) * gate_half],
                by_side(out_weight[0, :, side * out_half : (side + 1) * out_half], rows_in),
            ],
            axis=1,
        )

    lo, hi = packed(0), packed(1)
    keep = jnp.where(section == 0, lo, hi)
    got = swapped(jnp.where(section == 0, hi, lo))
    hops = hop_list()
    seat_bits = bits_of(n_seq)
    first, second = [
        Gather(
            jnp.where(section == layer, keep, got)[(None,) * len(hops)], list(range(len(hops)))
        )
        for layer in range(2)
    ]
    total_width = lo.shape[1]
    for bit in range(seat_bits):
        first.step()
    (inputs,) = stage([first, second], inputs[:, 0])
    hidden_bf = to_sequences(inputs, section, micro, n_seq)

    def three(job):
        end = mix_half + gate_half
        return [
            job.part(0, mix_half, False), job.part(mix_half, end, True),
            job.part(end, total_width, False),
        ]

    first_mix, first_gate, first_out = three(first)
    for job in (first_mix, first_gate, first_out):
        job.step()
    for bit in range(seat_bits // 2):
        second.step()

    def both_layers(array):
        other = swapped(array)
        lo = jnp.where(section == 0, array, other)
        hi = jnp.where(section == 0, other, array)
        return (lo[0], hi[0])

    sizes = [norm_gain, conv_weight.reshape(1, -1), conv_bias, dt_bias, a_log, d_skip, gated_gain]
    packed = jnp.concatenate(sizes, axis=1)
    splits = [int(s.shape[1]) for s in sizes]

    def unpack(flat):
        parts, at = [], 0
        for count in splits:
            parts.append(flat[at : at + count])
            at += count
        parts[1] = parts[1].reshape(conv_weight.shape[1:])
        return parts

    params = [unpack(flat) for flat in both_layers(packed)]
    length = lax.dynamic_index_in_dim(
        lax.dynamic_index_in_dim(seq_lengths, seat % micro, 0, keepdims=False), lane, 0,
        keepdims=False,
    )
    positions = run * tokens + jnp.arange(tokens)
    valid = (positions < length).astype(jnp.float32)[:, None]

    size = inner // heads
    lane_heads = lax.broadcasted_iota(jnp.int32, (inner, LANES), 0) // size
    heads_map = (lane_heads == lax.broadcasted_iota(jnp.int32, (inner, LANES), 1)).astype(
        jnp.bfloat16
    )

    def table(rows, wide):
        rows = [jnp.pad(row, (0, wide - row.shape[0])) for row in rows]
        return jnp.concatenate([jnp.stack(rows), jnp.zeros((8 - len(rows), wide), jnp.float32)])

    tables = []
    for gain_in, kernel, offset, dt_offset, alog, skip, gain_out in params:
        tables.append(
            (
                jnp.concatenate([kernel, offset[None], jnp.zeros((3, channels), jnp.float32)]),
                table([dt_offset, alog, skip], LANES),
                table([gain_out], inner),
            )
        )

    kept = []
    wholes = []
    layer_outs = []
    for layer in range(2):
        gain_in = params[layer][0]
        taps, head, gain = tables[layer]
        hidden = hidden_bf.astype(jnp.float32)
        normed_in = norm_rows(hidden, gain_in).astype(jnp.bfloat16)
        mix_job, gate_job, out_job = layer_jobs = (
            [first_mix, first_gate, first_out] if layer == 0 else second_jobs
        )
        own = mix_job.whole()
        mix_whole = Halves(own, swapped(own))
        xm = times(normed_in, mix_whole, section, jnp.bfloat16)
        halo = neighbour(xm[tokens - 16 :], run, seat, whole_run, -1)
        waits = []
        if layer == 0:
            for bit in range(seat_bits - seat_bits // 2):
                second.step()
            (xm,) = stage([second], xm)
            second_jobs = three(second)
        conv, enter, state, total = run_states(xm, halo, taps, head, inner, size, waits)
        into = carried(state, total, run, seat, whole_run, -1, size)
        if layer == 1:
            gate_job.step([total])
        own = gate_job.whole()
        gate_whole = Halves(own, swapped(own))
        out_job.step([total])
        own = by_rows(out_job.whole(), rows_in)
        out_whole = Halves(own, swapped(own))
        wholes.append((mix_whole, gate_whole, out_whole))
        gate = times(normed_in, gate_whole, section, jnp.bfloat16)
        if layer == 0:
            second_jobs[0].step()
            second_jobs[1].step()
            waits = arrays_of(second_jobs[:2])
        else:
            cot = to_sequences(
                later(cotangent, [first_flag])[:, 0], section, micro, n_seq, [total]
            )
            waits = [cot]
        whole, y, normed_out, flag = run_scan(
            conv, xm, enter, into, gate, head, gain, inner, size, waits
        )
        branch = times(normed_out, out_whole, section, jnp.float32)
        layer_out = (valid * (hidden + branch)).astype(jnp.bfloat16)
        if layer == 0:
            first_flag = flag
            second_jobs[2].step([flag])
            layer_out = second_jobs[0].step((), layer_out)
        kept.append((hidden_bf, normed_in, gate, xm, halo, conv, total, whole, y, normed_out))
        layer_outs.append(layer_out)
        hidden_bf = layer_out
    act_one = sent_pieces(half_pieces(layer_outs[0], section, micro), micro, n_seq)
    act_two = sent_pieces(half_pieces(layer_outs[1], section, micro), micro, n_seq)

    grad_bf = cot
    small = [None] * 2
    for layer in (1, 0):
        gain_in = params[layer][0]
        taps, head, gain = tables[layer]
        hid, normed_in, gate, xm, halo, conv, total, whole, y, normed_out = kept[layer]
        mix_whole, gate_whole, out_whole = wholes[layer]
        masked = grad_bf.astype(jnp.float32) * valid
        grad_branch = masked.astype(jnp.bfloat16)
        sum_out = Scatter(
            by_side(weight_sum(normed_out, grad_branch, section), rows_in), False
        )
        grad_normed = times_back(grad_branch, out_whole, section).astype(jnp.bfloat16)
        waits = []
        if layer == 0:
            two_gate.step()
            two_out.step()
            two_both = two_gate.joined(two_out)
            two_both.step()
            waits = [two_both.array, two_one.array, two_two.array]
        grad_y, grad_gate, gain_sum, left = run_gate(
            grad_normed, y, gate, conv, xm, head, gain, inner, size, waits
        )
        after = carried(left, total, run, seat, whole_run, 1, size)
        sum_gate = Scatter(weight_sum(normed_in, grad_gate, section), True)
        gate_part = times_back(grad_gate, gate_whole, section)
        waits = [sum_out.array, sum_gate.array, gate_part[:16, :LANES]]
        if layer == 0:
            two_both.step((), [gain_sum])
            two_one.step((), [gain_sum])
            two_two.step((), [gain_sum])
            waits = waits + [two_both.array, two_one.array, two_two.array]
        grad_mix, tap_sum, head_sum, edge = run_back(
            grad_y, conv, xm, halo, whole, after, taps, head, heads_map, inner, size, waits
        )
        sum_out.step((), [head_sum])
        sum_gate.step((), [head_sum])
        if layer == 0:
            two_one.step((), [head_sum])
            two_two.step((), [head_sum])
            edge, pieces_two = stage(
                [two_one, two_two, sum_out, sum_gate, two_both], edge, pieces_two
            )
        else:
            edge, act_one, act_two = stage([sum_out, sum_gate], edge, act_one, act_two)
        edge = neighbour(edge, run, seat, whole_run, 1)
        fixed_rows = grad_mix[tokens - 16 :, :channels].astype(jnp.float32) + jnp.pad(
            edge, ((8, 0), (0, 0))
        )
        grad_mix = lax.dynamic_update_slice(
            grad_mix, fixed_rows.astype(jnp.bfloat16), (tokens - 16, 0)
        )

        def mix_sums():
            half = weight_sum(normed_in, grad_mix, section)
            middle = half.shape[1] // 2
            return Scatter(half[:, :middle], False), Scatter(half[:, middle:], True)

        if layer == 0:
            sum_one, sum_two = mix_sums()
            (grad_mix,) = stage([sum_one, sum_two], grad_mix)
            two_mix = two_one.joined(two_two)
            for job in (sum_gate, sum_out, two_mix):
                job.step()
            one_both = sum_gate.joined(sum_out)
            for job in (sum_one, sum_two, one_both, two_mix):
                job.step()
        grad_normed_in = gate_part + times_back(grad_mix, mix_whole, section)
        if layer == 1:
            sum_one, sum_two = mix_sums()
        _, pull_norm = jax.vjp(norm_rows, hid.astype(jnp.float32), gain_in)
        grad_hidden, grad_gain_in = pull_norm(grad_normed_in)
        grad_bf = (masked + grad_hidden).astype(jnp.bfloat16)
        if layer == 0:
            (grad_bf,) = stage([sum_one, sum_two, one_both, two_mix], grad_bf)
        small[layer] = jnp.concatenate(
            [
                grad_gain_in, tap_sum[:4].reshape(-1), tap_sum[4], head_sum[0, :heads],
                head_sum[1, :heads], head_sum[2, :heads], gain_sum[0],
            ]
        )
        pieces = half_pieces(grad_bf, section, micro)
        if layer == 1:
            pieces_two = sent_pieces(pieces, micro, n_seq)
            two_gate, two_out, two_one, two_two = sum_gate, sum_out, sum_one, sum_two
    pieces_one = sent_pieces(pieces, micro, n_seq)
    mine = jnp.where(section == 0, small[0], small[1])
    others = jnp.where(section == 0, small[1], small[0])
    small_sum = mine + swapped(others)
    small_hops = hop_list()[::-1]
    for job in (sum_one, sum_two, one_both, two_mix):
        job.step()
    one_mix = sum_one.joined(sum_two)
    (small_sum,) = stage([one_mix, one_both, two_mix], small_sum)
    while one_mix.order:
        one_mix.step()
        one_both.step()
        for axis, distance in small_hops[:2]:
            small_sum = small_sum + exchanged(small_sum, axis, distance)
        small_hops = small_hops[2:]
        if len(one_mix.order) == 1:
            small_sum, pieces_one = stage([one_mix], small_sum, pieces_one)
    for axis, distance in small_hops:
        small_sum = small_sum + exchanged(small_sum, axis, distance)
    one = jnp.concatenate([one_both.shard(), one_mix.shard()], axis=1)
    two = jnp.concatenate([two_both.shard(), two_mix.shard()], axis=1)
    keep = jnp.where(section == 0, one, two)
    other = swapped(jnp.where(section == 0, two, one))
    lo = jnp.where(section == 0, keep, other).astype(jnp.float32)
    hi = jnp.where(section == 0, other, keep).astype(jnp.float32)
    ends = [gate_half, gate_half + 2 * out_half]
    grad_in_weight = jnp.concatenate(
        [lo[:, : ends[0]], hi[:, : ends[0]], lo[:, ends[1] :], hi[:, ends[1] :]], axis=1
    )[:, :proj]
    grad_out_weight = jnp.concatenate(
        [by_rows(lo[:, ends[0] : ends[1]], rows_in), by_rows(hi[:, ends[0] : ends[1]], rows_in)],
        axis=1,
    )
    acts = whole_pieces(act_one, act_two, section)
    grads = whole_pieces(pieces_one, pieces_two, section)
    g = unpack(small_sum)
    g[3] = g[3] + nothing_of(seen)[:heads]
    return (
        acts[None, :, None],
        grads[None, :, None],
        g[0][None],
        grad_in_weight[None],
        g[1][None],
        g[2][None],
        g[3][None],
        g[4][None],
        g[5][None],
        g[6][None],
        grad_out_weight[None],
    )


def solution(mesh):
    return jax.shard_map(
        local,
        mesh=mesh,
        in_specs=(
            P(None, "wshard", "seq", None),
            P(),
            P(None, "wshard", "seq", None),
            P("section", None),
            P("section", ("seq", "wshard"), None),
            P("section", None, None),
            P("section", None),
            P("section", None),
            P("section", None),
            P("section", None),
            P("section", None),
            P("section", ("seq", "wshard"), None),
        ),
        out_specs=(
            P("section", None, "wshard", "seq", None),
            P("section", None, "wshard", "seq", None),
            P("section", None),
            P("section", ("seq", "wshard"), None),
            P("section", None, None),
            P("section", None),
            P("section", None),
            P("section", None),
            P("section", None),
            P("section", None),
            P("section", ("seq", "wshard"), None),
        ),
        check_vma=False,
    )
```
